1024 devices in a mesh: gz: 64 (over y, x), ha: 16 (over z, core).
Axes of the slice: x: 8, y: 8, z: 8, core: 2. Of those that a mesh axis runs over, the one named last changes fastest.
Arguments:
- source: float32 [128, 512, 512], P('gz', 'ha'), may hold values from -5 to 5
- faces: float32 [129], replicated, may hold values from 1000 to 8000
Outputs:
- pressure: float32 [128, 512, 512], P('gz', 'ha')
The draws below stay inside these ranges and needn't reach their ends.
All inputs are finite; a program needn't handle non-finite values.
Results may differ from the reference program's by a relative error of at most 0.00095.
Values sent between devices are 32-bit elements; how exact they have to be, the bound alone decides.
No kernel may reach another device: no remote copies, remote signals or barrier semaphores. Data moves between devices by JAX's collectives and lax.ppermute only.
A program may use at most 128 MiB of HBM per device.

```python
import math
import jax
import jax.numpy as jnp
from jax import lax

NX = 512
NY = 512
NZ = 128


def draw_source(key, part):
    key = jax.random.fold_in(key, 11)
    return jnp.clip(jax.random.normal(key, (NZ, NY, NX), jnp.float32), -5.0, 5.0)


def setup_inputs(seed: int = 0) -> dict:
    key_list = jax.random.split(jax.random.key(seed), 3)
    source = draw_source(jax.random.fold_in(key_list[2], 71), 0)
    faces = jnp.clip(jnp.exp(jax.random.uniform(key_list[1], (NZ + 1,), jnp.float32, math.log(1000.0), math.log(8000.0))), 1000.0, 8000.0)
    return dict(source=source, faces=faces)


HIGH = lax.Precision.HIGHEST

def hartley(count):
    index = jnp.arange(count, dtype=jnp.int32)
    phase = (index[:, None] * index[None, :] % count).astype(jnp.float32) * (2.0 * math.pi / count)
    return (jnp.cos(phase) + jnp.sin(phase)) / math.sqrt(count)

def eigen(index, count):
    return 2.0 - 2.0 * jnp.cos(index.astype(jnp.float32) * (2.0 * math.pi / count))

def forward_sweep(lower, upper, rhs, shift, start_c, start_d):

    def forward(carry, row):
        cprime, dprime = carry
        low, up, value = row
        pivot = low + up + shift + low * cprime
        cnext = -up / pivot
        dnext = (value + low * dprime) / pivot
        return ((cnext, dnext), (cnext, dnext))
    final, (cseq, dseq) = lax.scan(forward, (start_c, start_d), (lower, upper, rhs))
    return (cseq, dseq)

def back_sweep(cseq, dseq, above):

    def backward(carry, row):
        cvalue, dvalue = row
        value = dvalue - cvalue * carry
        return (value, value)
    final, solved = lax.scan(backward, above, (cseq, dseq), reverse=True)
    return solved

def reference(source, faces):
    hx = hartley(NX)
    hy = hartley(NY)
    half = jnp.einsum('zyx,xk->zky', source, hx, precision=HIGH)
    modes = jnp.einsum('zky,yl->zkl', half, hy, precision=HIGH)
    shift = eigen(jnp.arange(NX, dtype=jnp.int32), NX)[:, None] + eigen(jnp.arange(NY, dtype=jnp.int32), NY)[None, :]
    zero = jnp.zeros((NX, NY), jnp.float32)
    cseq, dseq = forward_sweep(faces[:-1], faces[1:], modes, shift, zero, zero)
    solved = back_sweep(cseq, dseq, zero)
    back = jnp.einsum('zkl,ly->zky', solved, hy, precision=HIGH)
    return jnp.einsum('zky,kx->zyx', back, hx, precision=HIGH)
```

```python
import math

import jax
import jax.numpy as jnp
import ml_dtypes
import numpy as np
from jax import lax
from jax.experimental import pallas as pl
from jax.experimental.pallas import tpu as pltpu
from jax.sharding import Mesh, PartitionSpec as P

N = 512
M = N // 2
NZ = 128
BY = 8
BX = 8
HA = 16
BLOCK = NZ // BY
F32 = jnp.float32
BF16 = jnp.bfloat16


def tables():
    j = np.arange(M)
    def cas(phase):
        t = 2.0 * np.pi * (phase % N) / N
        return (np.cos(t) + np.sin(t)) / math.sqrt(N)
    even = cas(2 * j[:, None] * j[None, :])
    odd = cas((2 * j[:, None] + 1) * j[None, :])
    def split(a):
        hi = a.astype(ml_dtypes.bfloat16)
        return [hi, (a - hi.astype(np.float64)).astype(ml_dtypes.bfloat16)]
    forward = np.stack(split(even) + split(odd.T))
    inverse = np.stack(split(even) + split(odd))
    eigen = 2.0 - 2.0 * np.cos(2.0 * np.pi * np.arange(N) / N)
    parity = (np.arange(8) // 2) % 2
    eigen_y = eigen[2 * j[None, :] + parity[:, None]]
    return forward, inverse, eigen.astype(np.float32), eigen_y.astype(np.float32)


def product(value, high, low):
    top = value.astype(BF16)
    rest = (value - top.astype(F32)).astype(BF16)
    rows = value.shape[0]
    both = jnp.dot(jnp.concatenate([top, rest], 0), high, preferred_element_type=F32)
    return both[:rows] + both[rows:] + jnp.dot(top, low, preferred_element_type=F32)


def swap_blocks(value):
    sub = lax.broadcasted_iota(jnp.int32, value.shape, 1) // 2
    lane = lax.broadcasted_iota(jnp.int32, value.shape, 2) // 32
    which = (sub - lane) & 3
    out = value
    for s in range(1, 4):
        moved = pltpu.roll(pltpu.roll(value, 2 * s, 1), 128 - 32 * s, 2)
        out = jnp.where(which == s, moved, out)
    return out


def first_of_pair(shape):
    return ((lax.broadcasted_iota(jnp.int32, shape, 1) // 2) & 1) == 0


def forward_x(source, table, out):
    value = source[...]
    left, right = value[:, :M], value[:, M:]
    even = product(left + right, table[0], table[1])
    odd = product(left - right, table[2], table[3])
    out[...] = jnp.concatenate([even, odd], 0).T


def inverse_x(spectral, table, out):
    value = spectral[...].T
    even = product(value[:64], table[0], table[1])
    odd = product(value[64:], table[2], table[3])
    out[:, :M] = even + odd
    out[:, M:] = even - odd


def coefficients(faces, eigen, eigen_y, up_out, down_out, weight_out, ups, downs):
    first = 4 * (lax.axis_index("x") * HA + lax.axis_index("h"))
    sub = lax.broadcasted_iota(jnp.int32, (8, M), 0)
    wave = 2 * (sub & 1) + (sub >> 2)
    shift = eigen_y[...]
    for e in range(4):
        shift = shift + jnp.where(wave == e, eigen[first + e], 0.0)

    def inv(index):
        return 1.0 / jnp.full((8, M), faces[index], F32)

    def steps(i, carry):
        p, u, q, w = carry
        for k in range(8):
            z = i * 8 + k
            p = p + inv(z) * u
            u = u + shift * p
            ups[z] = p
            q = q + inv(NZ - z) * w
            w = w + shift * q
            downs[NZ - 1 - z] = q
        return p, u, q, w

    zero = jnp.zeros((8, M), F32)
    one = jnp.ones((8, M), F32)
    p, u, q, w = lax.fori_loop(0, NZ // 8, steps, (zero, one, zero, one))
    weight_out[...] = 1.0 / (p + inv(NZ) * u)
    base = lax.axis_index("y") * BLOCK
    up_out[...] = ups[pl.ds(base, BLOCK)]
    down_out[...] = downs[pl.ds(base, BLOCK)]


def forward_y(received, table, ups, downs, weight, local, sums):
    value = received[...].reshape(BX, 2, 2, 8, 128)
    low, high = value[:, 0], value[:, 1]

    def lines(part):
        part = swap_blocks(part.reshape(BX * 2, 8, 128)).reshape(BX, 2, 8, 128)
        return jnp.concatenate([part[:, 0].reshape(64, 128), part[:, 1].reshape(64, 128)], 1)

    even = product(lines(low + high), table[0], table[1]).reshape(BX, 8, M)
    odd = product(lines(low - high), table[2], table[3]).reshape(BX, 8, M)
    mask = first_of_pair((BX, 8, M))
    scale = weight[...]
    lower = jnp.where(mask, even, pltpu.roll(odd, 2, 1)) * scale
    upper = jnp.where(mask, pltpu.roll(even, 6, 1), odd) * scale
    rows = [(lower if j % 2 == 0 else upper)[j // 2] for j in range(BLOCK)]
    above = [None] * BLOCK
    total_q = jnp.zeros((8, M), F32)
    for j in reversed(range(BLOCK)):
        above[j] = total_q
        total_q = total_q + downs[j] * rows[j]
    total_p = jnp.zeros((8, M), F32)
    for j in range(BLOCK):
        total_p = total_p + ups[j] * rows[j]
        local[j] = downs[j] * total_p + ups[j] * above[j]
    me = lax.axis_index("y")
    for b in range(BY):
        sums[b] = jnp.where(b > me, total_p, total_q)


def inverse_y(local, ups, downs, sums, table, out):
    me = lax.axis_index("y")
    below = jnp.zeros((8, M), F32)
    above = jnp.zeros((8, M), F32)
    for b in range(BY):
        below = below + jnp.where(b < me, sums[b], 0.0)
        above = above + jnp.where(b > me, sums[b], 0.0)
    value = local[...] + downs[...] * below + ups[...] * above
    value = value.reshape(BX, 2, 8, M)
    lower, upper = value[:, 0], value[:, 1]
    mask = first_of_pair((BX, 8, M))
    even = jnp.where(mask, lower, pltpu.roll(upper, 2, 1)).reshape(64, M)
    odd = jnp.where(mask, pltpu.roll(lower, 6, 1), upper).reshape(64, M)
    even = product(even, table[0], table[1])
    odd = product(odd, table[2], table[3])
    for half, part in enumerate((even + odd, even - odd)):
        for side in range(2):
            piece = part[:, side * 128 : (side + 1) * 128].reshape(BX, 8, 128)
            out[:, half, side] = swap_blocks(piece)


def shape(*dims):
    return jax.ShapeDtypeStruct(dims, F32)


VMEM = pl.BlockSpec(memory_space=pltpu.VMEM)
SMEM = pl.BlockSpec(memory_space=pltpu.SMEM)


def on_device(source, faces):
    forward, inverse, eigen, eigen_y = (jnp.asarray(t) for t in tables())
    with jax.named_scope("coefficients"):
        ups, downs, weight = pl.pallas_call(
            coefficients,
            out_shape=(shape(BLOCK, 8, M), shape(BLOCK, 8, M), shape(8, M)),
            in_specs=[SMEM, SMEM, VMEM],
            out_specs=(VMEM, VMEM, VMEM),
            scratch_shapes=[pltpu.VMEM((NZ, 8, M), F32), pltpu.VMEM((NZ, 8, M), F32)],
        )(faces, eigen, eigen_y)
    with jax.named_scope("forward_x"):
        half = pl.pallas_call(
            forward_x, out_shape=shape(M, 128), in_specs=[VMEM, VMEM], out_specs=VMEM
        )(source.reshape(64, N), forward)
    with jax.named_scope("exchange_out"):
        pencils = lax.all_to_all(half.reshape(BX * HA, 2, 128), ("x", "h"), 0, 0, tiled=True)
    with jax.named_scope("forward_y"):
        local, sums = pl.pallas_call(
            forward_y,
            out_shape=(shape(BLOCK, 8, M), shape(BY, 8, M)),
            in_specs=[VMEM] * 5,
            out_specs=(VMEM, VMEM),
        )(pencils.reshape(M, 128), forward, ups, downs, weight)
    with jax.named_scope("exchange_sums"):
        sums = lax.all_to_all(sums, "y", 0, 0, tiled=True)
    with jax.named_scope("inverse_y"):
        back = pl.pallas_call(
            inverse_y,
            out_shape=shape(BX, 2, 2, 8, 128),
            in_specs=[VMEM] * 5,
            out_specs=VMEM,
        )(local, ups, downs, sums, inverse)
    with jax.named_scope("exchange_back"):
        grid = lax.all_to_all(back.reshape(BX * HA, 2, 128), ("x", "h"), 0, 0, tiled=True)
    with jax.named_scope("inverse_x"):
        out = pl.pallas_call(
            inverse_x, out_shape=shape(64, N), in_specs=[VMEM, VMEM], out_specs=VMEM
        )(grid.reshape(M, 128), inverse)
    return out.reshape(2, 32, N)


def solution(mesh):
    fine = Mesh(mesh.devices.reshape(BY, BX, HA), ("y", "x", "h"))
    return jax.shard_map(
        on_device,
        mesh=fine,
        in_specs=(P(("y", "x"), "h", None), P()),
        out_specs=P(("y", "x"), "h", None),
        check_vma=False,
    )
```

```python
import math

import jax
import jax.numpy as jnp
import ml_dtypes
import numpy as np
from jax import lax
from jax.experimental import pallas as pl
from jax.experimental.pallas import tpu as pltpu
from jax.sharding import Mesh, PartitionSpec as P

N = 512
M = N // 2
NZ = 128
BY = 8
BX = 8
HA = 16
BLOCK = NZ // BY
F32 = jnp.float32
BF16 = jnp.bfloat16


def tables():
    j = np.arange(M)
    def cas(phase):
        t = 2.0 * np.pi * (phase % N) / N
        return (np.cos(t) + np.sin(t)) / math.sqrt(N)
    even = cas(2 * j[:, None] * j[None, :])
    odd = cas((2 * j[:, None] + 1) * j[None, :])
    def split(a):
        hi = a.astype(ml_dtypes.bfloat16)
        return [hi, (a - hi.astype(np.float64)).astype(ml_dtypes.bfloat16)]
    forward = np.stack(split(even) + split(odd.T))
    inverse = np.stack(split(even) + split(odd))
    eigen = 2.0 - 2.0 * np.cos(2.0 * np.pi * np.arange(N) / N)
    parity = (np.arange(8) // 2) % 2
    eigen_y = eigen[2 * j[None, :] + parity[:, None]]
    return forward, inverse, eigen.astype(np.float32), eigen_y.astype(np.float32)


def product(value, high, low):
    top = value.astype(BF16)
    rest = (value - top.astype(F32)).astype(BF16)
    rows = value.shape[0]
    both = jnp.dot(jnp.concatenate([top, rest], 0), high, preferred_element_type=F32)
    return both[:rows] + both[rows:] + jnp.dot(top, low, preferred_element_type=F32)


def swap_blocks(value):
    sub = lax.broadcasted_iota(jnp.int32, value.shape, 1) // 2
    lane = lax.broadcasted_iota(jnp.int32, value.shape, 2) // 32
    which = (sub - lane) & 3
    out = value
    for s in range(1, 4):
        moved = pltpu.roll(pltpu.roll(value, 2 * s, 1), 128 - 32 * s, 2)
        out = jnp.where(which == s, moved, out)
    return out


def first_of_pair(shape):
    return ((lax.broadcasted_iota(jnp.int32, shape, 1) // 2) & 1) == 0


def forward_x(source, table, out):
    value = source[...]
    left, right = value[:, :M], value[:, M:]
    even = product(left + right, table[0], table[1])
    odd = product(left - right, table[2], table[3])
    out[...] = jnp.concatenate([even, odd], 0).T


def inverse_x(spectral, table, out):
    value = spectral[...].T
    even = product(value[:64], table[0], table[1])
    odd = product(value[64:], table[2], table[3])
    out[:, :M] = even + odd
    out[:, M:] = even - odd


def coefficients(faces, eigen, eigen_y, up_out, down_out, weight_out, ups, downs):
    first = 4 * (lax.axis_index("x") * HA + lax.axis_index("h"))
    sub = lax.broadcasted_iota(jnp.int32, (8, M), 0)
    wave = 2 * (sub & 1) + (sub >> 2)
    shift = eigen_y[...]
    for e in range(4):
        shift = shift + jnp.where(wave == e, eigen[first + e], 0.0)

    def inv(index):
        return 1.0 / jnp.full((8, M), faces[index], F32)

    def steps(i, carry):
        p, u, q, w = carry
        for k in range(8):
            z = i * 8 + k
            p = p + inv(z) * u
            u = u + shift * p
            ups[z] = p
            q = q + inv(NZ - z) * w
            w = w + shift * q
            downs[NZ - 1 - z] = q
        return p, u, q, w

    zero = jnp.zeros((8, M), F32)
    one = jnp.ones((8, M), F32)
    p, u, q, w = lax.fori_loop(0, NZ // 8, steps, (zero, one, zero, one))
    weight_out[...] = 1.0 / (p + inv(NZ) * u)
    base = lax.axis_index("y") * BLOCK
    up_out[...] = ups[pl.ds(base, BLOCK)]
    down_out[...] = downs[pl.ds(base, BLOCK)]


def forward_y(received, table, ups, downs, weight, local, sums):
    value = received[...].reshape(BX, 2, 2, 8, 128)
    low, high = value[:, 0], value[:, 1]

    def lines(part):
        part = swap_blocks(part.reshape(BX * 2, 8, 128)).reshape(BX, 2, 8, 128)
        return jnp.concatenate([part[:, 0].reshape(64, 128), part[:, 1].reshape(64, 128)], 1)

    even = product(lines(low + high), table[0], table[1]).reshape(BX, 8, M)
    odd = product(lines(low - high), table[2], table[3]).reshape(BX, 8, M)
    mask = first_of_pair((BX, 8, M))
    scale = weight[...]
    lower = jnp.where(mask, even, pltpu.roll(odd, 2, 1)) * scale
    upper = jnp.where(mask, pltpu.roll(even, 6, 1), odd) * scale
    rows = [(lower if j % 2 == 0 else upper)[j // 2] for j in range(BLOCK)]
    above = [None] * BLOCK
    total_q = jnp.zeros((8, M), F32)
    for j in reversed(range(BLOCK)):
        above[j] = total_q
        total_q = total_q + downs[j] * rows[j]
    total_p = jnp.zeros((8, M), F32)
    for j in range(BLOCK):
        total_p = total_p + ups[j] * rows[j]
        local[j] = downs[j] * total_p + ups[j] * above[j]
    me = lax.axis_index("y")
    for b in range(BY):
        sums[b] = jnp.where(b > me, total_p, total_q)


def inverse_y(local, ups, downs, sums, table, out):
    me = lax.axis_index("y")
    below = jnp.zeros((8, M), F32)
    above = jnp.zeros((8, M), F32)
    for b in range(BY):
        below = below + jnp.where(b < me, sums[b], 0.0)
        above = above + jnp.where(b > me, sums[b], 0.0)
    value = local[...] + downs[...] * below + ups[...] * above
    value = value.reshape(BX, 2, 8, M)
    lower, upper = value[:, 0], value[:, 1]
    mask = first_of_pair((BX, 8, M))
    even = jnp.where(mask, lower, pltpu.roll(upper, 2, 1)).reshape(64, M)
    odd = jnp.where(mask, pltpu.roll(lower, 6, 1), upper).reshape(64, M)
    even = product(even, table[0], table[1])
    odd = product(odd, table[2], table[3])
    for half, part in enumerate((even + odd, even - odd)):
        for side in range(2):
            piece = part[:, side * 128 : (side + 1) * 128].reshape(BX, 8, 128)
            out[:, half, side] = swap_blocks(piece)


def shape(*dims):
    return jax.ShapeDtypeStruct(dims, F32)


VMEM = pl.BlockSpec(memory_space=pltpu.VMEM)
SMALL = pltpu.CompilerParams(vmem_limit_bytes=8 * 1024 * 1024)
SMEM = pl.BlockSpec(memory_space=pltpu.SMEM)


def on_device(source, faces):
    forward, inverse, eigen, eigen_y = (jnp.asarray(t) for t in tables())
    with jax.named_scope("coefficients"):
        ups, downs, weight = pl.pallas_call(
            coefficients,
            out_shape=(shape(BLOCK, 8, M), shape(BLOCK, 8, M), shape(8, M)),
            in_specs=[SMEM, SMEM, VMEM],
            out_specs=(VMEM, VMEM, VMEM),
            scratch_shapes=[pltpu.VMEM((NZ, 8, M), F32), pltpu.VMEM((NZ, 8, M), F32)],
            compiler_params=SMALL,
        )(faces, eigen, eigen_y)
    with jax.named_scope("forward_x"):
        half = pl.pallas_call(
            forward_x,
            out_shape=shape(M, 128),
            in_specs=[VMEM, VMEM],
            out_specs=VMEM,
            compiler_params=SMALL,
        )(source.reshape(64, N), forward)
    with jax.named_scope("exchange_out"):
        pencils = lax.all_to_all(half.reshape(BX * HA, 2, 128), ("x", "h"), 0, 0, tiled=True)
    with jax.named_scope("forward_y"):
        local, sums = pl.pallas_call(
            forward_y,
            out_shape=(shape(BLOCK, 8, M), shape(BY, 8, M)),
            in_specs=[VMEM] * 5,
            out_specs=(VMEM, VMEM),
            compiler_params=SMALL,
        )(pencils.reshape(M, 128), forward, ups, downs, weight)
    with jax.named_scope("exchange_sums"):
        sums = lax.all_to_all(sums, "y", 0, 0, tiled=True)
    with jax.named_scope("inverse_y"):
        back = pl.pallas_call(
            inverse_y,
            out_shape=shape(BX, 2, 2, 8, 128),
            in_specs=[VMEM] * 5,
            out_specs=VMEM,
            compiler_params=SMALL,
        )(local, ups, downs, sums, inverse)
    with jax.named_scope("exchange_back"):
        grid = lax.all_to_all(back.reshape(BX * HA, 2, 128), ("x", "h"), 0, 0, tiled=True)
    with jax.named_scope("inverse_x"):
        out = pl.pallas_call(
            inverse_x,
            out_shape=shape(64, N),
            in_specs=[VMEM, VMEM],
            out_specs=VMEM,
            compiler_params=SMALL,
        )(grid.reshape(M, 128), inverse)
    return out.reshape(2, 32, N)


def solution(mesh):
    fine = Mesh(mesh.devices.reshape(BY, BX, HA), ("y", "x", "h"))
    return jax.shard_map(
        on_device,
        mesh=fine,
        in_specs=(P(("y", "x"), "h", None), P()),
        out_specs=P(("y", "x"), "h", None),
        check_vma=False,
    )
```

```python
import math

import jax
import jax.numpy as jnp
import ml_dtypes
import numpy as np
from jax import lax
from jax.experimental import pallas as pl
from jax.experimental.pallas import tpu as pltpu
from jax.sharding import Mesh, PartitionSpec as P

N = 512
M = N // 2
NZ = 128
BY = 8
BX = 8
HA = 16
BLOCK = NZ // BY
F32 = jnp.float32
BF16 = jnp.bfloat16


def tables():
    j = np.arange(M)
    def cas(phase):
        t = 2.0 * np.pi * (phase % N) / N
        return (np.cos(t) + np.sin(t)) / math.sqrt(N)
    even = cas(2 * j[:, None] * j[None, :])
    odd = cas((2 * j[:, None] + 1) * j[None, :])
    def split(a):
        hi = a.astype(ml_dtypes.bfloat16)
        return [hi, (a - hi.astype(np.float64)).astype(ml_dtypes.bfloat16)]
    forward = np.stack(split(even) + split(odd.T))
    inverse = np.stack(split(even) + split(odd))
    eigen = 2.0 - 2.0 * np.cos(2.0 * np.pi * np.arange(N) / N)
    parity = (np.arange(8) // 2) % 2
    eigen_y = eigen[2 * j[None, :] + parity[:, None]]
    return forward, inverse, eigen.astype(np.float32), eigen_y.astype(np.float32)


def product(value, high, low):
    top = value.astype(BF16)
    rest = (value - top.astype(F32)).astype(BF16)
    rows = value.shape[0]
    both = jnp.dot(jnp.concatenate([top, rest], 0), high, preferred_element_type=F32)
    return both[:rows] + both[rows:] + jnp.dot(top, low, preferred_element_type=F32)


def swap_blocks(value):
    sub = lax.broadcasted_iota(jnp.int32, value.shape, 1) // 2
    lane = lax.broadcasted_iota(jnp.int32, value.shape, 2) // 32
    which = (sub - lane) & 3
    out = value
    for s in range(1, 4):
        moved = pltpu.roll(pltpu.roll(value, 2 * s, 1), 128 - 32 * s, 2)
        out = jnp.where(which == s, moved, out)
    return out


def first_of_pair(shape):
    return ((lax.broadcasted_iota(jnp.int32, shape, 1) // 2) & 1) == 0


def first_kernel(
    source, table, faces, eigen, eigen_y, half, up_out, down_out, weight_out,
    value, matrix, face, wave, wave_y, below_p, below_u, above_q, above_w, sems,
):
    copies = [
        pltpu.make_async_copy(src, dst, sems.at[n])
        for n, (src, dst) in enumerate(
            ((faces, face), (eigen, wave), (eigen_y, wave_y), (source, value), (table, matrix))
        )
    ]
    for copy in copies:
        copy.start()
    for copy in copies[:3]:
        copy.wait()
    coefficients(
        face, wave, wave_y, up_out, down_out, weight_out, below_p, below_u, above_q, above_w
    )
    for copy in copies[3:]:
        copy.wait()
    left, right = value[:, :M], value[:, M:]
    even = product(left + right, matrix[0], matrix[1])
    odd = product(left - right, matrix[2], matrix[3])
    half[...] = jnp.concatenate([even, odd], 0).T


def inverse_x(spectral, table, out):
    value = spectral[...].T
    even = product(value[:64], table[0], table[1])
    odd = product(value[64:], table[2], table[3])
    out[:, :M] = even + odd
    out[:, M:] = even - odd


def coefficients(faces, eigen, eigen_y, up_out, down_out, weight_out, ps, us, qs, ws):
    first = 4 * (lax.axis_index("x") * HA + lax.axis_index("h"))
    sub = lax.broadcasted_iota(jnp.int32, (8, M), 0)
    wave = 2 * (sub & 1) + (sub >> 2)
    shift = eigen_y[...]
    for e in range(4):
        shift = shift + jnp.where(wave == e, eigen[first + e], 0.0)

    def inv(index):
        half = 1.0 / jnp.full((8, 128), faces[index], F32)
        return jnp.concatenate([half, half], 1)

    blocks = []
    for b in range(BY):
        g = inv(b * BLOCK)
        pa, ua = jnp.ones((8, M), F32), shift
        pb, ub = g, 1.0 + shift * g
        for j in range(1, BLOCK):
            g = inv(b * BLOCK + j)
            pa = pa + g * ua
            ua = ua + shift * pa
            pb = pb + g * ub
            ub = ub + shift * pb
        blocks.append((pa, pb, ua, ub))
    p, u = jnp.zeros((8, M), F32), jnp.ones((8, M), F32)
    for b in range(BY):
        ps[b], us[b] = p, u
        pa, pb, ua, ub = blocks[b]
        p, u = pa * p + pb * u, ua * p + ub * u
    last = inv(NZ)
    weight_out[...] = 1.0 / (p + last * u)
    q, w = last, jnp.ones((8, M), F32)
    for b in reversed(range(BY)):
        qs[b], ws[b] = q, w
        pa, pb, ua, ub = blocks[b]
        q, w = ub * q + pb * w, ua * q + pa * w

    me = lax.axis_index("y")
    inner = [inv(me * BLOCK + j) for j in range(BLOCK)]
    p, u = ps[me], us[me]
    q, w = qs[me], ws[me]
    for j in range(BLOCK):
        p = p + inner[j] * u
        up_out[j] = p
        u = u + shift * p
        k = BLOCK - 1 - j
        down_out[k] = q
        w = w + shift * q
        q = q + inner[k] * w


def forward_y(received, table, ups, downs, weight, local, sums):
    value = received[...].reshape(BX, 2, 2, 8, 128)
    low, high = value[:, 0], value[:, 1]

    def lines(part):
        part = swap_blocks(part.reshape(BX * 2, 8, 128)).reshape(BX, 2, 8, 128)
        return jnp.concatenate([part[:, 0].reshape(64, 128), part[:, 1].reshape(64, 128)], 1)

    even = product(lines(low + high), table[0], table[1]).reshape(BX, 8, M)
    odd = product(lines(low - high), table[2], table[3]).reshape(BX, 8, M)
    mask = first_of_pair((BX, 8, M))
    scale = weight[...]
    lower = jnp.where(mask, even, pltpu.roll(odd, 2, 1)) * scale
    upper = jnp.where(mask, pltpu.roll(even, 6, 1), odd) * scale
    rows = [(lower if j % 2 == 0 else upper)[j // 2] for j in range(BLOCK)]
    above = [None] * BLOCK
    total_q = jnp.zeros((8, M), F32)
    for j in reversed(range(BLOCK)):
        above[j] = total_q
        total_q = total_q + downs[j] * rows[j]
    total_p = jnp.zeros((8, M), F32)
    for j in range(BLOCK):
        total_p = total_p + ups[j] * rows[j]
        local[j] = downs[j] * total_p + ups[j] * above[j]
    me = lax.axis_index("y")
    for b in range(BY):
        sums[b] = jnp.where(b > me, total_p, total_q)


def inverse_y(local, ups, downs, sums, table, out):
    me = lax.axis_index("y")
    below = jnp.zeros((8, M), F32)
    above = jnp.zeros((8, M), F32)
    for b in range(BY):
        below = below + jnp.where(b < me, sums[b], 0.0)
        above = above + jnp.where(b > me, sums[b], 0.0)
    value = local[...] + downs[...] * below + ups[...] * above
    value = value.reshape(BX, 2, 8, M)
    lower, upper = value[:, 0], value[:, 1]
    mask = first_of_pair((BX, 8, M))
    even = jnp.where(mask, lower, pltpu.roll(upper, 2, 1)).reshape(64, M)
    odd = jnp.where(mask, pltpu.roll(lower, 6, 1), upper).reshape(64, M)
    even = product(even, table[0], table[1])
    odd = product(odd, table[2], table[3])
    for half, part in enumerate((even + odd, even - odd)):
        for side in range(2):
            piece = part[:, side * 128 : (side + 1) * 128].reshape(BX, 8, 128)
            out[:, half, side] = swap_blocks(piece)


def shape(*dims):
    return jax.ShapeDtypeStruct(dims, F32)


VMEM = pl.BlockSpec(memory_space=pltpu.VMEM)
SMALL = pltpu.CompilerParams(vmem_limit_bytes=8 * 1024 * 1024)
HBM = pl.BlockSpec(memory_space=pltpu.HBM)


def on_device(source, faces):
    forward, inverse, eigen, eigen_y = (jnp.asarray(t) for t in tables())
    with jax.named_scope("forward_x"):
        half, ups, downs, weight = pl.pallas_call(
            first_kernel,
            out_shape=(shape(M, 128), shape(BLOCK, 8, M), shape(BLOCK, 8, M), shape(8, M)),
            in_specs=[HBM] * 5,
            out_specs=(VMEM,) * 4,
            scratch_shapes=[
                pltpu.VMEM((64, N), F32),
                pltpu.VMEM((4, M, M), BF16),
                pltpu.SMEM((NZ + 1,), F32),
                pltpu.SMEM((N,), F32),
                pltpu.VMEM((8, M), F32),
                pltpu.VMEM((BY, 8, M), F32),
                pltpu.VMEM((BY, 8, M), F32),
                pltpu.VMEM((BY, 8, M), F32),
                pltpu.VMEM((BY, 8, M), F32),
                pltpu.SemaphoreType.DMA((5,)),
            ],
            compiler_params=SMALL,
        )(source.reshape(64, N), forward, faces, eigen, eigen_y)
    with jax.named_scope("exchange_out"):
        pencils = lax.all_to_all(half.reshape(BX * HA, 2, 128), ("x", "h"), 0, 0, tiled=True)
    with jax.named_scope("forward_y"):
        local, sums = pl.pallas_call(
            forward_y,
            out_shape=(shape(BLOCK, 8, M), shape(BY, 8, M)),
            in_specs=[VMEM] * 5,
            out_specs=(VMEM, VMEM),
            compiler_params=SMALL,
        )(pencils.reshape(M, 128), forward, ups, downs, weight)
    with jax.named_scope("exchange_sums"):
        sums = lax.all_to_all(sums, "y", 0, 0, tiled=True)
    with jax.named_scope("inverse_y"):
        back = pl.pallas_call(
            inverse_y,
            out_shape=shape(BX, 2, 2, 8, 128),
            in_specs=[VMEM] * 5,
            out_specs=VMEM,
            compiler_params=SMALL,
        )(local, ups, downs, sums, inverse)
    with jax.named_scope("exchange_back"):
        grid = lax.all_to_all(back.reshape(BX * HA, 2, 128), ("x", "h"), 0, 0, tiled=True)
    with jax.named_scope("inverse_x"):
        out = pl.pallas_call(
            inverse_x,
            out_shape=shape(64, N),
            in_specs=[VMEM, VMEM],
            out_specs=VMEM,
            compiler_params=SMALL,
        )(grid.reshape(M, 128), inverse)
    return out.reshape(2, 32, N)


def solution(mesh):
    fine = Mesh(mesh.devices.reshape(BY, BX, HA), ("y", "x", "h"))
    return jax.shard_map(
        on_device,
        mesh=fine,
        in_specs=(P(("y", "x"), "h", None), P()),
        out_specs=P(("y", "x"), "h", None),
        check_vma=False,
    )
```

```python
import math

import jax
import jax.numpy as jnp
import ml_dtypes
import numpy as np
from jax import lax
from jax.experimental import pallas as pl
from jax.experimental.pallas import tpu as pltpu
from jax.sharding import Mesh, PartitionSpec as P

N = 512
M = N // 2
NZ = 128
BY = 8
BX = 8
HA = 16
BLOCK = NZ // BY
F32 = jnp.float32
BF16 = jnp.bfloat16


def tables():
    j = np.arange(M)
    def cas(phase):
        t = 2.0 * np.pi * (phase % N) / N
        return (np.cos(t) + np.sin(t)) / math.sqrt(N)
    even = cas(2 * j[:, None] * j[None, :])
    odd = cas((2 * j[:, None] + 1) * j[None, :])
    def split(a):
        hi = a.astype(ml_dtypes.bfloat16)
        return [hi, (a - hi.astype(np.float64)).astype(ml_dtypes.bfloat16)]
    forward = np.stack(split(even) + split(odd.T))
    inverse = np.stack(split(even) + split(odd))
    eigen = 2.0 - 2.0 * np.cos(2.0 * np.pi * np.arange(N) / N)
    parity = (np.arange(8) // 2) % 2
    eigen_y = eigen[2 * j[None, :] + parity[:, None]]
    return forward, inverse, eigen.astype(np.float32), eigen_y.astype(np.float32)


def product(value, high, low):
    top = value.astype(BF16)
    rest = (value - top.astype(F32)).astype(BF16)
    rows = value.shape[0]
    both = jnp.dot(jnp.concatenate([top, rest], 0), high, preferred_element_type=F32)
    return both[:rows] + both[rows:] + jnp.dot(top, low, preferred_element_type=F32)


def swap_blocks(value):
    sub = lax.broadcasted_iota(jnp.int32, value.shape, 1) // 2
    lane = lax.broadcasted_iota(jnp.int32, value.shape, 2) // 32
    which = (sub - lane) & 3
    out = value
    for s in range(1, 4):
        moved = pltpu.roll(pltpu.roll(value, 2 * s, 1), 128 - 32 * s, 2)
        out = jnp.where(which == s, moved, out)
    return out


def first_of_pair(shape):
    return ((lax.broadcasted_iota(jnp.int32, shape, 1) // 2) & 1) == 0


def forward_x(source, table, out):
    value = source[...]
    left, right = value[:, :M], value[:, M:]
    even = product(left + right, table[0], table[1])
    odd = product(left - right, table[2], table[3])
    out[...] = jnp.concatenate([even, odd], 0).T


def inverse_x(spectral, table, out):
    value = spectral[...].T
    even = product(value[:64], table[0], table[1])
    odd = product(value[64:], table[2], table[3])
    out[:, :M] = even + odd
    out[:, M:] = even - odd


def coefficients(faces, eigen, eigen_y, up_out, down_out, weight_out, ups, downs):
    first = 4 * (lax.axis_index("x") * HA + lax.axis_index("h"))
    sub = lax.broadcasted_iota(jnp.int32, (8, M), 0)
    wave = 2 * (sub & 1) + (sub >> 2)
    shift = eigen_y[...]
    for e in range(4):
        shift = shift + jnp.where(wave == e, eigen[first + e], 0.0)

    def inv(index):
        return 1.0 / jnp.full((8, M), faces[index], F32)

    def steps(i, carry):
        p, u, q, w = carry
        for k in range(8):
            z = i * 8 + k
            p = p + inv(z) * u
            u = u + shift * p
            ups[z] = p
            q = q + inv(NZ - z) * w
            w = w + shift * q
            downs[NZ - 1 - z] = q
        return p, u, q, w

    zero = jnp.zeros((8, M), F32)
    one = jnp.ones((8, M), F32)
    p, u, q, w = lax.fori_loop(0, NZ // 8, steps, (zero, one, zero, one))
    weight_out[...] = 1.0 / (p + inv(NZ) * u)
    base = lax.axis_index("y") * BLOCK
    up_out[...] = ups[pl.ds(base, BLOCK)]
    down_out[...] = downs[pl.ds(base, BLOCK)]


def forward_y(received, table, ups, downs, weight, local, sums):
    value = received[...].reshape(BX, 2, 2, 8, 128)
    low, high = value[:, 0], value[:, 1]

    def lines(part):
        part = swap_blocks(part.reshape(BX * 2, 8, 128)).reshape(BX, 2, 8, 128)
        return jnp.concatenate([part[:, 0].reshape(64, 128), part[:, 1].reshape(64, 128)], 1)

    even = product(lines(low + high), table[0], table[1]).reshape(BX, 8, M)
    odd = product(lines(low - high), table[2], table[3]).reshape(BX, 8, M)
    mask = first_of_pair((BX, 8, M))
    scale = weight[...]
    lower = jnp.where(mask, even, pltpu.roll(odd, 2, 1)) * scale
    upper = jnp.where(mask, pltpu.roll(even, 6, 1), odd) * scale
    rows = [(lower if j % 2 == 0 else upper)[j // 2] for j in range(BLOCK)]
    above = [None] * BLOCK
    total_q = jnp.zeros((8, M), F32)
    for j in reversed(range(BLOCK)):
        above[j] = total_q
        total_q = total_q + downs[j] * rows[j]
    total_p = jnp.zeros((8, M), F32)
    for j in range(BLOCK):
        total_p = total_p + ups[j] * rows[j]
        local[j] = downs[j] * total_p + ups[j] * above[j]
    me = lax.axis_index("y")
    for b in range(BY):
        sums[b] = jnp.where(b > me, total_p, total_q)


def inverse_y(local, ups, downs, sums, table, out):
    me = lax.axis_index("y")
    below = jnp.zeros((8, M), F32)
    above = jnp.zeros((8, M), F32)
    for b in range(BY):
        below = below + jnp.where(b < me, sums[b], 0.0)
        above = above + jnp.where(b > me, sums[b], 0.0)
    value = local[...] + downs[...] * below + ups[...] * above
    value = value.reshape(BX, 2, 8, M)
    lower, upper = value[:, 0], value[:, 1]
    mask = first_of_pair((BX, 8, M))
    even = jnp.where(mask, lower, pltpu.roll(upper, 2, 1)).reshape(64, M)
    odd = jnp.where(mask, pltpu.roll(lower, 6, 1), upper).reshape(64, M)
    even = product(even, table[0], table[1])
    odd = product(odd, table[2], table[3])
    for half, part in enumerate((even + odd, even - odd)):
        for side in range(2):
            piece = part[:, side * 128 : (side + 1) * 128].reshape(BX, 8, 128)
            out[:, half, side] = swap_blocks(piece)


def shape(*dims):
    return jax.ShapeDtypeStruct(dims, F32)


VMEM = pl.BlockSpec(memory_space=pltpu.VMEM)
SMALL = pltpu.CompilerParams(vmem_limit_bytes=8 * 1024 * 1024)
SMEM = pl.BlockSpec(memory_space=pltpu.SMEM)


def on_device(source, faces):
    forward, inverse, eigen, eigen_y = (jnp.asarray(t) for t in tables())
    with jax.named_scope("coefficients"):
        ups, downs, weight = pl.pallas_call(
            coefficients,
            out_shape=(shape(BLOCK, 8, M), shape(BLOCK, 8, M), shape(8, M)),
            in_specs=[SMEM, SMEM, VMEM],
            out_specs=(VMEM, VMEM, VMEM),
            scratch_shapes=[pltpu.VMEM((NZ, 8, M), F32), pltpu.VMEM((NZ, 8, M), F32)],
            compiler_params=SMALL,
        )(faces, eigen, eigen_y)
    with jax.named_scope("forward_x"):
        half = pl.pallas_call(
            forward_x,
            out_shape=shape(M, 128),
            in_specs=[VMEM, VMEM],
            out_specs=VMEM,
        )(source.reshape(64, N), forward)
    with jax.named_scope("exchange_out"):
        pencils = lax.all_to_all(half.reshape(BX * HA, 2, 128), ("x", "h"), 0, 0, tiled=True)
    with jax.named_scope("forward_y"):
        local, sums = pl.pallas_call(
            forward_y,
            out_shape=(shape(BLOCK, 8, M), shape(BY, 8, M)),
            in_specs=[VMEM] * 5,
            out_specs=(VMEM, VMEM),
            compiler_params=SMALL,
        )(pencils.reshape(M, 128), forward, ups, downs, weight)
    with jax.named_scope("exchange_sums"):
        sums = lax.all_to_all(sums, "y", 0, 0, tiled=True)
    with jax.named_scope("inverse_y"):
        back = pl.pallas_call(
            inverse_y,
            out_shape=shape(BX, 2, 2, 8, 128),
            in_specs=[VMEM] * 5,
            out_specs=VMEM,
            compiler_params=SMALL,
        )(local, ups, downs, sums, inverse)
    with jax.named_scope("exchange_back"):
        grid = lax.all_to_all(back.reshape(BX * HA, 2, 128), ("x", "h"), 0, 0, tiled=True)
    with jax.named_scope("inverse_x"):
        out = pl.pallas_call(
            inverse_x,
            out_shape=shape(64, N),
            in_specs=[VMEM, VMEM],
            out_specs=VMEM,
            compiler_params=SMALL,
        )(grid.reshape(M, 128), inverse)
    return out.reshape(2, 32, N)


def solution(mesh):
    fine = Mesh(mesh.devices.reshape(BY, BX, HA), ("y", "x", "h"))
    return jax.shard_map(
        on_device,
        mesh=fine,
        in_specs=(P(("y", "x"), "h", None), P()),
        out_specs=P(("y", "x"), "h", None),
        check_vma=False,
    )
```

```python
import math

import jax
import jax.numpy as jnp
import ml_dtypes
import numpy as np
from jax import lax
from jax.experimental import pallas as pl
from jax.experimental.pallas import tpu as pltpu
from jax.sharding import Mesh, PartitionSpec as P

N = 512
M = N // 2
NZ = 128
NY = 8
NX = 8
BX = 4
BLOCKS = NZ // (2 * BX)
BLOCK = NZ // BLOCKS
HA = 16
WAVES = N // (BX * HA)
F32 = jnp.float32
BF16 = jnp.bfloat16


def tables():
    j = np.arange(M)
    def cas(phase):
        t = 2.0 * np.pi * (phase % N) / N
        return (np.cos(t) + np.sin(t)) / math.sqrt(N)
    even = cas(2 * j[:, None] * j[None, :])
    odd = cas((2 * j[:, None] + 1) * j[None, :])
    def split(a):
        hi = a.astype(ml_dtypes.bfloat16)
        return [hi, (a - hi.astype(np.float64)).astype(ml_dtypes.bfloat16)]
    forward = np.stack(split(even) + split(odd.T))
    inverse = np.stack(split(even) + split(odd))
    eigen = 2.0 - 2.0 * np.cos(2.0 * np.pi * np.arange(N) / N)
    parity = (np.arange(16) // 4) % 2
    eigen_y = eigen[2 * j[None, :] + parity[:, None]]
    return forward, inverse, eigen.astype(np.float32), eigen_y.astype(np.float32)


def product(value, high, low):
    top = value.astype(BF16)
    rest = (value - top.astype(F32)).astype(BF16)
    rows = value.shape[0]
    both = jnp.dot(jnp.concatenate([top, rest], 0), high, preferred_element_type=F32)
    return both[:rows] + both[rows:] + jnp.dot(top, low, preferred_element_type=F32)


def swap_blocks(value):
    row = lax.broadcasted_iota(jnp.int32, value.shape, 1) // 4
    lane = lax.broadcasted_iota(jnp.int32, value.shape, 2) // 32
    which = (row - lane) & 3
    out = value
    for s in range(1, 4):
        moved = pltpu.roll(pltpu.roll(value, 4 * s, 1), 128 - 32 * s, 2)
        out = jnp.where(which == s, moved, out)
    return out


def lower_half(shape):
    return lax.broadcasted_iota(jnp.int32, shape, 1) < 4


def place(index):
    return index + lax.axis_index("x1") * (BX - 1 - 2 * index)


def own_block():
    return 2 * lax.axis_index("y") + lax.axis_index("x1")


def block_at(position):
    return 2 * (position % NY) + position // NY


def forward_x(source, table, out):
    value = source[...]
    left, right = value[:, :M], value[:, M:]
    even = product(left + right, table[0], table[1])
    odd = product(left - right, table[2], table[3])
    half = jnp.concatenate([even, odd], 0).T
    for share in range(BX):
        out[pl.ds(place(share) * 64, 64)] = half[share * 64 : (share + 1) * 64]


def inverse_x(spectral, table, out):
    shares = [spectral[pl.ds(place(share) * 64, 64)] for share in range(BX)]
    value = jnp.concatenate(shares, 0).T
    even = product(value[:64], table[0], table[1])
    odd = product(value[64:], table[2], table[3])
    out[:, :M] = even + odd
    out[:, M:] = even - odd


def coefficients(faces, eigen, eigen_y, up_out, down_out, weight_out, ups, downs):
    first = WAVES * (place(lax.axis_index("x2")) * HA + lax.axis_index("h"))
    row = lax.broadcasted_iota(jnp.int32, (16, M), 0)
    wave = 2 * (row & 3) + (row >> 3)
    shift = eigen_y[...]
    for e in range(WAVES):
        shift = shift + jnp.where(wave == e, eigen[first + e], 0.0)

    def inv(index):
        part = 1.0 / jnp.full((8, 128), faces[index], F32)
        part = jnp.concatenate([part, part], 1)
        return jnp.concatenate([part, part], 0)

    def steps(i, carry):
        p, u, q, w = carry
        for k in range(8):
            z = i * 8 + k
            p = p + inv(z) * u
            u = u + shift * p
            ups[z] = p
            q = q + inv(NZ - z) * w
            w = w + shift * q
            downs[NZ - 1 - z] = q
        return p, u, q, w

    zero = jnp.zeros((16, M), F32)
    one = jnp.ones((16, M), F32)
    p, u, q, w = lax.fori_loop(0, NZ // 8, steps, (zero, one, zero, one))
    weight_out[...] = 1.0 / (p + inv(NZ) * u)
    base = own_block() * BLOCK
    up_out[...] = ups[pl.ds(base, BLOCK)]
    down_out[...] = downs[pl.ds(base, BLOCK)]


def forward_y(received, table, ups, downs, weight, local, sums):
    value = received[...].reshape(BX, 2, 2, 16, 128)
    low, high = value[:, 0], value[:, 1]

    def lines(part):
        part = swap_blocks(part.reshape(BX * 2, 16, 128)).reshape(BX, 2, 16, 128)
        return jnp.concatenate([part[:, 0].reshape(64, 128), part[:, 1].reshape(64, 128)], 1)

    even = product(lines(low + high), table[0], table[1]).reshape(8, 8, M)
    odd = product(lines(low - high), table[2], table[3]).reshape(8, 8, M)
    mask = lower_half((8, 8, M))
    lower = jnp.where(mask, even, pltpu.roll(odd, 4, 1)).reshape(BX, 16, M)
    upper = jnp.where(mask, pltpu.roll(even, 4, 1), odd).reshape(BX, 16, M)
    scale = weight[...]
    rows = [(lower if j % 2 == 0 else upper)[j // 2] * scale for j in range(BLOCK)]
    above = [None] * BLOCK
    total_q = jnp.zeros((16, M), F32)
    for j in reversed(range(BLOCK)):
        above[j] = total_q
        total_q = total_q + downs[j] * rows[j]
    total_p = jnp.zeros((16, M), F32)
    for j in range(BLOCK):
        total_p = total_p + ups[j] * rows[j]
        local[j] = downs[j] * total_p + ups[j] * above[j]
    me = own_block()
    for n in range(BLOCKS):
        sums[n] = jnp.where(block_at(n) > me, total_p, total_q)


def inverse_y(local, ups, downs, sums, table, out):
    me = own_block()
    below = jnp.zeros((16, M), F32)
    above = jnp.zeros((16, M), F32)
    for n in range(BLOCKS):
        below = below + jnp.where(block_at(n) < me, sums[n], 0.0)
        above = above + jnp.where(block_at(n) > me, sums[n], 0.0)
    value = local[...] + downs[...] * below + ups[...] * above
    value = value.reshape(BX, 2, 16, M)
    lower, upper = value[:, 0].reshape(8, 8, M), value[:, 1].reshape(8, 8, M)
    mask = lower_half((8, 8, M))
    even = jnp.where(mask, lower, pltpu.roll(upper, 4, 1)).reshape(64, M)
    odd = jnp.where(mask, pltpu.roll(lower, 4, 1), upper).reshape(64, M)
    even = product(even, table[0], table[1])
    odd = product(odd, table[2], table[3])
    for half, part in enumerate((even + odd, even - odd)):
        for side in range(2):
            piece = part[:, side * 128 : (side + 1) * 128].reshape(BX, 16, 128)
            out[:, half, side] = swap_blocks(piece)


def shape(*dims):
    return jax.ShapeDtypeStruct(dims, F32)


VMEM = pl.BlockSpec(memory_space=pltpu.VMEM)
SMALL = pltpu.CompilerParams(vmem_limit_bytes=12 * 1024 * 1024)
SMEM = pl.BlockSpec(memory_space=pltpu.SMEM)


def on_device(source, faces):
    forward, inverse, eigen, eigen_y = (jnp.asarray(t) for t in tables())
    with jax.named_scope("coefficients"):
        ups, downs, weight = pl.pallas_call(
            coefficients,
            out_shape=(shape(BLOCK, 16, M), shape(BLOCK, 16, M), shape(16, M)),
            in_specs=[SMEM, SMEM, VMEM],
            out_specs=(VMEM, VMEM, VMEM),
            scratch_shapes=[pltpu.VMEM((NZ, 16, M), F32), pltpu.VMEM((NZ, 16, M), F32)],
            compiler_params=SMALL,
        )(faces, eigen, eigen_y)
    with jax.named_scope("forward_x"):
        half = pl.pallas_call(
            forward_x,
            out_shape=shape(M, 128),
            in_specs=[VMEM, VMEM],
            out_specs=VMEM,
        )(source.reshape(64, N), forward)
    with jax.named_scope("exchange_out"):
        pencils = lax.all_to_all(half.reshape(BX * HA, 4, 128), ("x2", "h"), 0, 0, tiled=True)
    with jax.named_scope("forward_y"):
        local, sums = pl.pallas_call(
            forward_y,
            out_shape=(shape(BLOCK, 16, M), shape(BLOCKS, 16, M)),
            in_specs=[VMEM] * 5,
            out_specs=(VMEM, VMEM),
            compiler_params=SMALL,
        )(pencils.reshape(M, 128), forward, ups, downs, weight)
    with jax.named_scope("exchange_sums"):
        groups = [[y * NX + x for x in (k, NX - 1 - k) for y in range(NY)] for k in range(BX)]
        sums = lax.all_to_all(
            sums, ("y", "x1", "x2"), 0, 0, tiled=True, axis_index_groups=groups
        )
    with jax.named_scope("inverse_y"):
        back = pl.pallas_call(
            inverse_y,
            out_shape=shape(BX, 2, 2, 16, 128),
            in_specs=[VMEM] * 5,
            out_specs=VMEM,
            compiler_params=SMALL,
        )(local, ups, downs, sums, inverse)
    with jax.named_scope("exchange_back"):
        grid = lax.all_to_all(back.reshape(BX * HA, 4, 128), ("x2", "h"), 0, 0, tiled=True)
    with jax.named_scope("inverse_x"):
        out = pl.pallas_call(
            inverse_x,
            out_shape=shape(64, N),
            in_specs=[VMEM, VMEM],
            out_specs=VMEM,
            compiler_params=SMALL,
        )(grid.reshape(M, 128), inverse)
    return out.reshape(2, 32, N)


def solution(mesh):
    fine = Mesh(mesh.devices.reshape(NY, 2, BX, HA), ("y", "x1", "x2", "h"))
    spec = P(("y", "x1", "x2"), "h", None)
    return jax.shard_map(
        on_device, mesh=fine, in_specs=(spec, P()), out_specs=spec, check_vma=False
    )
```

```python
import math

import jax
import jax.numpy as jnp
import ml_dtypes
import numpy as np
from jax import lax
from jax.experimental import pallas as pl
from jax.experimental.pallas import tpu as pltpu
from jax.sharding import Mesh, PartitionSpec as P

N = 512
M = N // 2
NZ = 128
NY = 8
NX = 8
BX = 4
BLOCKS = NZ // (2 * BX)
BLOCK = NZ // BLOCKS
HA = 16
WAVES = N // (BX * HA)
F32 = jnp.float32
BF16 = jnp.bfloat16


def tables():
    j = np.arange(M)
    def cas(phase):
        t = 2.0 * np.pi * (phase % N) / N
        return (np.cos(t) + np.sin(t)) / math.sqrt(N)
    even = cas(2 * j[:, None] * j[None, :])
    odd = cas((2 * j[:, None] + 1) * j[None, :])
    def split(a):
        hi = a.astype(ml_dtypes.bfloat16)
        return [hi, (a - hi.astype(np.float64)).astype(ml_dtypes.bfloat16)]
    forward = np.stack(split(even) + split(odd.T))
    inverse = np.stack(split(even) + split(odd))
    eigen = 2.0 - 2.0 * np.cos(2.0 * np.pi * np.arange(N) / N)
    parity = (np.arange(16) // 4) % 2
    eigen_y = eigen[2 * j[None, :] + parity[:, None]]
    return forward, inverse, eigen.astype(np.float32), eigen_y.astype(np.float32)


def product(value, high, low):
    top = value.astype(BF16)
    rest = (value - top.astype(F32)).astype(BF16)
    rows = value.shape[0]
    both = jnp.dot(jnp.concatenate([top, rest], 0), high, preferred_element_type=F32)
    return both[:rows] + both[rows:] + jnp.dot(top, low, preferred_element_type=F32)


def swap_blocks(value):
    row = lax.broadcasted_iota(jnp.int32, value.shape, 1) // 4
    lane = lax.broadcasted_iota(jnp.int32, value.shape, 2) // 32
    which = (row - lane) & 3
    out = value
    for s in range(1, 4):
        moved = pltpu.roll(pltpu.roll(value, 4 * s, 1), 128 - 32 * s, 2)
        out = jnp.where(which == s, moved, out)
    return out


def lower_half(shape):
    return lax.broadcasted_iota(jnp.int32, shape, 1) < 4


def place(index):
    return index + lax.axis_index("x1") * (BX - 1 - 2 * index)


def own_block():
    return 2 * lax.axis_index("y") + lax.axis_index("x1")


def block_at(position):
    return 2 * (position % NY) + position // NY


def forward_x(
    source, matrices, faces, eigen, eigen_y, out, up_out, down_out, weight_out,
    value, table, face, wave_x, wave_y, ps, us, qs, ws, sems,
):
    copies = [
        pltpu.make_async_copy(src, dst, sems.at[n])
        for n, (src, dst) in enumerate(
            ((faces, face), (eigen, wave_x), (eigen_y, wave_y), (source, value), (matrices, table))
        )
    ]
    for copy in copies:
        copy.start()
    for copy in copies[:3]:
        copy.wait()
    coefficients(face, wave_x, wave_y, up_out, down_out, weight_out, ps, us, qs, ws)
    for copy in copies[3:]:
        copy.wait()
    left, right = value[:, :M], value[:, M:]
    even = product(left + right, table[0], table[1])
    odd = product(left - right, table[2], table[3])
    half = jnp.concatenate([even, odd], 0).T
    for share in range(BX):
        out[pl.ds(place(share) * 64, 64)] = half[share * 64 : (share + 1) * 64]


def inverse_x(spectral, table, out):
    shares = [spectral[pl.ds(place(share) * 64, 64)] for share in range(BX)]
    value = jnp.concatenate(shares, 0).T
    even = product(value[:64], table[0], table[1])
    odd = product(value[64:], table[2], table[3])
    out[:, :M] = even + odd
    out[:, M:] = even - odd


def coefficients(faces, eigen, eigen_y, up_out, down_out, weight_out, ps, us, qs, ws):
    first = WAVES * (place(lax.axis_index("x2")) * HA + lax.axis_index("h"))
    row = lax.broadcasted_iota(jnp.int32, (16, M), 0)
    wave = 2 * (row & 3) + (row >> 3)
    shift = eigen_y[...]
    for e in range(WAVES):
        shift = shift + jnp.where(wave == e, eigen[first + e], 0.0)

    def inv(index):
        part = 1.0 / jnp.full((8, 128), faces[index], F32)
        part = jnp.concatenate([part, part], 1)
        return jnp.concatenate([part, part], 0)

    blocks = [None] * BLOCKS
    for b in range(0, BLOCKS, 2):
        for c in (b, b + 1):
            g = inv(c * BLOCK)
            blocks[c] = (jnp.ones((16, M), F32), g, shift, 1.0 + shift * g)
        for j in range(1, BLOCK):
            for c in (b, b + 1):
                pa, pb, ua, ub = blocks[c]
                g = inv(c * BLOCK + j)
                pa, pb = pa + g * ua, pb + g * ub
                blocks[c] = (pa, pb, ua + shift * pa, ub + shift * pb)
    last = inv(NZ)
    p, u = jnp.zeros((16, M), F32), jnp.ones((16, M), F32)
    q, w = last, jnp.ones((16, M), F32)
    for b in range(BLOCKS):
        ps[b], us[b] = p, u
        pa, pb, ua, ub = blocks[b]
        p, u = pa * p + pb * u, ua * p + ub * u
        c = BLOCKS - 1 - b
        qs[c], ws[c] = q, w
        pa, pb, ua, ub = blocks[c]
        q, w = ub * q + pb * w, ua * q + pa * w
    weight_out[...] = 1.0 / (p + last * u)

    me = own_block()
    inner = [inv(me * BLOCK + j) for j in range(BLOCK)]
    p, u, q, w = ps[me], us[me], qs[me], ws[me]
    for j in range(BLOCK):
        p = p + inner[j] * u
        up_out[j] = p
        u = u + shift * p
        k = BLOCK - 1 - j
        down_out[k] = q
        w = w + shift * q
        q = q + inner[k] * w


def forward_y(received, table, ups, downs, weight, local, sums):
    value = received[...].reshape(BX, 2, 2, 16, 128)
    low, high = value[:, 0], value[:, 1]

    def lines(part):
        part = swap_blocks(part.reshape(BX * 2, 16, 128)).reshape(BX, 2, 16, 128)
        return jnp.concatenate([part[:, 0].reshape(64, 128), part[:, 1].reshape(64, 128)], 1)

    even = product(lines(low + high), table[0], table[1]).reshape(8, 8, M)
    odd = product(lines(low - high), table[2], table[3]).reshape(8, 8, M)
    mask = lower_half((8, 8, M))
    lower = jnp.where(mask, even, pltpu.roll(odd, 4, 1)).reshape(BX, 16, M)
    upper = jnp.where(mask, pltpu.roll(even, 4, 1), odd).reshape(BX, 16, M)
    scale = weight[...]
    rows = [(lower if j % 2 == 0 else upper)[j // 2] * scale for j in range(BLOCK)]
    above = [None] * BLOCK
    total_q = jnp.zeros((16, M), F32)
    for j in reversed(range(BLOCK)):
        above[j] = total_q
        total_q = total_q + downs[j] * rows[j]
    total_p = jnp.zeros((16, M), F32)
    for j in range(BLOCK):
        total_p = total_p + ups[j] * rows[j]
        local[j] = downs[j] * total_p + ups[j] * above[j]
    me = own_block()
    for n in range(BLOCKS):
        sums[n] = jnp.where(block_at(n) > me, total_p, total_q)


def inverse_y(local, ups, downs, sums, table, out):
    me = own_block()
    below = jnp.zeros((16, M), F32)
    above = jnp.zeros((16, M), F32)
    for n in range(BLOCKS):
        below = below + jnp.where(block_at(n) < me, sums[n], 0.0)
        above = above + jnp.where(block_at(n) > me, sums[n], 0.0)
    value = local[...] + downs[...] * below + ups[...] * above
    value = value.reshape(BX, 2, 16, M)
    lower, upper = value[:, 0].reshape(8, 8, M), value[:, 1].reshape(8, 8, M)
    mask = lower_half((8, 8, M))
    even = jnp.where(mask, lower, pltpu.roll(upper, 4, 1)).reshape(64, M)
    odd = jnp.where(mask, pltpu.roll(lower, 4, 1), upper).reshape(64, M)
    even = product(even, table[0], table[1])
    odd = product(odd, table[2], table[3])
    for half, part in enumerate((even + odd, even - odd)):
        for side in range(2):
            piece = part[:, side * 128 : (side + 1) * 128].reshape(BX, 16, 128)
            out[:, half, side] = swap_blocks(piece)


def shape(*dims):
    return jax.ShapeDtypeStruct(dims, F32)


VMEM = pl.BlockSpec(memory_space=pltpu.VMEM)
SMALL = pltpu.CompilerParams(vmem_limit_bytes=12 * 1024 * 1024)
HBM = pl.BlockSpec(memory_space=pltpu.HBM)


def on_device(source, faces):
    forward, inverse, eigen, eigen_y = (jnp.asarray(t) for t in tables())
    with jax.named_scope("forward_x"):
        operands = (source.reshape(64, N), forward, faces, eigen, eigen_y)
        half, ups, downs, weight = pl.pallas_call(
            forward_x,
            out_shape=(shape(M, 128), shape(BLOCK, 16, M), shape(BLOCK, 16, M), shape(16, M)),
            in_specs=[HBM] * 5,
            out_specs=(VMEM,) * 4,
            scratch_shapes=[
                pltpu.VMEM((64, N), F32),
                pltpu.VMEM((4, M, M), BF16),
                pltpu.SMEM((NZ + 1,), F32),
                pltpu.SMEM((N,), F32),
                pltpu.VMEM((16, M), F32),
                *[pltpu.VMEM((BLOCKS, 16, M), F32)] * 4,
                pltpu.SemaphoreType.DMA((5,)),
            ],
            compiler_params=SMALL,
        )(*[pltpu.with_memory_space_constraint(x, pltpu.HBM) for x in operands])
    with jax.named_scope("exchange_out"):
        pencils = lax.all_to_all(half.reshape(BX * HA, 4, 128), ("x2", "h"), 0, 0, tiled=True)
    with jax.named_scope("forward_y"):
        local, sums = pl.pallas_call(
            forward_y,
            out_shape=(shape(BLOCK, 16, M), shape(BLOCKS, 16, M)),
            in_specs=[VMEM] * 5,
            out_specs=(VMEM, VMEM),
            compiler_params=SMALL,
        )(pencils.reshape(M, 128), forward, ups, downs, weight)
    with jax.named_scope("exchange_sums"):
        groups = [[y * NX + x for x in (k, NX - 1 - k) for y in range(NY)] for k in range(BX)]
        sums = lax.all_to_all(
            sums, ("y", "x1", "x2"), 0, 0, tiled=True, axis_index_groups=groups
        )
    with jax.named_scope("inverse_y"):
        back = pl.pallas_call(
            inverse_y,
            out_shape=shape(BX, 2, 2, 16, 128),
            in_specs=[VMEM] * 5,
            out_specs=VMEM,
            compiler_params=SMALL,
        )(local, ups, downs, sums, inverse)
    with jax.named_scope("exchange_back"):
        grid = lax.all_to_all(back.reshape(BX * HA, 4, 128), ("x2", "h"), 0, 0, tiled=True)
    with jax.named_scope("inverse_x"):
        out = pl.pallas_call(
            inverse_x,
            out_shape=shape(64, N),
            in_specs=[VMEM, VMEM],
            out_specs=VMEM,
            compiler_params=SMALL,
        )(grid.reshape(M, 128), inverse)
    return out.reshape(2, 32, N)


def solution(mesh):
    fine = Mesh(mesh.devices.reshape(NY, 2, BX, HA), ("y", "x1", "x2", "h"))
    spec = P(("y", "x1", "x2"), "h", None)
    return jax.shard_map(
        on_device, mesh=fine, in_specs=(spec, P()), out_specs=spec, check_vma=False
    )
```

```python
import math

import jax
import jax.numpy as jnp
import ml_dtypes
import numpy as np
from jax import lax
from jax.experimental import pallas as pl
from jax.experimental.pallas import tpu as pltpu
from jax.sharding import Mesh, PartitionSpec as P

N = 512
M = N // 2
NZ = 128
NY = 8
NX = 8
BX = 4
BLOCKS = NZ // (2 * BX)
BLOCK = NZ // BLOCKS
HA = 16
WAVES = N // (BX * HA)
F32 = jnp.float32
BF16 = jnp.bfloat16


def tables():
    j = np.arange(M)
    def cas(phase):
        t = 2.0 * np.pi * (phase % N) / N
        return (np.cos(t) + np.sin(t)) / math.sqrt(N)
    even = cas(2 * j[:, None] * j[None, :])
    odd = cas((2 * j[:, None] + 1) * j[None, :])
    def split(a):
        hi = a.astype(ml_dtypes.bfloat16)
        return [hi, (a - hi.astype(np.float64)).astype(ml_dtypes.bfloat16)]
    forward = np.stack(split(even) + split(odd.T))
    inverse = np.stack(split(even) + split(odd))
    eigen = 2.0 - 2.0 * np.cos(2.0 * np.pi * np.arange(N) / N)
    parity = (np.arange(16) // 4) % 2
    eigen_y = eigen[2 * j[None, :] + parity[:, None]]
    return forward, inverse, eigen.astype(np.float32), eigen_y.astype(np.float32)


def product(value, high, low):
    top = value.astype(BF16)
    rest = (value - top.astype(F32)).astype(BF16)
    rows = value.shape[0]
    both = jnp.dot(jnp.concatenate([top, rest], 0), high, preferred_element_type=F32)
    return both[:rows] + both[rows:] + jnp.dot(top, low, preferred_element_type=F32)


def swap_blocks(value):
    row = lax.broadcasted_iota(jnp.int32, value.shape, 1) // 4
    lane = lax.broadcasted_iota(jnp.int32, value.shape, 2) // 32
    which = (row - lane) & 3
    out = value
    for s in range(1, 4):
        moved = pltpu.roll(pltpu.roll(value, 4 * s, 1), 128 - 32 * s, 2)
        out = jnp.where(which == s, moved, out)
    return out


def lower_half(shape):
    return lax.broadcasted_iota(jnp.int32, shape, 1) < 4


def place(index):
    return index + lax.axis_index("x1") * (BX - 1 - 2 * index)


def own_block():
    return 2 * lax.axis_index("y") + lax.axis_index("x1")


def block_at(position):
    return 2 * (position % NY) + position // NY


def forward_x(
    source, matrices, faces, eigen, eigen_y, out, up_out, down_out, weight_out, table,
    value, face, wave_x, wave_y, ps, us, qs, ws, sems,
):
    copies = [
        pltpu.make_async_copy(src, dst, sems.at[n])
        for n, (src, dst) in enumerate(
            ((faces, face), (eigen, wave_x), (eigen_y, wave_y), (source, value), (matrices, table))
        )
    ]
    for copy in copies:
        copy.start()
    for copy in copies[:3]:
        copy.wait()
    shift, blocks, inv = block_matrices(face, wave_x, wave_y)
    for copy in copies[3:]:
        copy.wait()
    left, right = value[:, :M], value[:, M:]
    even = product(left + right, table[0], table[1])
    odd = product(left - right, table[2], table[3])
    half = jnp.concatenate([even, odd], 0).T
    for share in range(BX):
        out[pl.ds(place(share) * 64, 64)] = half[share * 64 : (share + 1) * 64]
    coefficients(shift, blocks, inv, up_out, down_out, weight_out, ps, us, qs, ws)


def inverse_x(spectral, table, out):
    shares = [spectral[pl.ds(place(share) * 64, 64)] for share in range(BX)]
    value = jnp.concatenate(shares, 0).T
    even = product(value[:64], table[0], table[1])
    odd = product(value[64:], table[2], table[3])
    out[:, :M] = even + odd
    out[:, M:] = even - odd


def block_matrices(faces, eigen, eigen_y):
    first = WAVES * (place(lax.axis_index("x2")) * HA + lax.axis_index("h"))
    row = lax.broadcasted_iota(jnp.int32, (16, M), 0)
    wave = 2 * (row & 3) + (row >> 3)
    shift = eigen_y[...]
    for e in range(WAVES):
        shift = shift + jnp.where(wave == e, eigen[first + e], 0.0)

    def inv(index):
        part = 1.0 / jnp.full((8, 128), faces[index], F32)
        part = jnp.concatenate([part, part], 1)
        return jnp.concatenate([part, part], 0)

    blocks = [None] * BLOCKS
    for b in range(0, BLOCKS, 2):
        for c in (b, b + 1):
            g = inv(c * BLOCK)
            blocks[c] = (jnp.ones((16, M), F32), g, shift, 1.0 + shift * g)
        for j in range(1, BLOCK):
            for c in (b, b + 1):
                pa, pb, ua, ub = blocks[c]
                g = inv(c * BLOCK + j)
                pa, pb = pa + g * ua, pb + g * ub
                blocks[c] = (pa, pb, ua + shift * pa, ub + shift * pb)
    return shift, blocks, inv


def coefficients(shift, blocks, inv, up_out, down_out, weight_out, ps, us, qs, ws):
    last = inv(NZ)
    p, u = jnp.zeros((16, M), F32), jnp.ones((16, M), F32)
    q, w = last, jnp.ones((16, M), F32)
    for b in range(BLOCKS):
        ps[b], us[b] = p, u
        pa, pb, ua, ub = blocks[b]
        p, u = pa * p + pb * u, ua * p + ub * u
        c = BLOCKS - 1 - b
        qs[c], ws[c] = q, w
        pa, pb, ua, ub = blocks[c]
        q, w = ub * q + pb * w, ua * q + pa * w
    weight_out[...] = 1.0 / (p + last * u)

    me = own_block()
    inner = [inv(me * BLOCK + j) for j in range(BLOCK)]
    p, u, q, w = ps[me], us[me], qs[me], ws[me]
    for j in range(BLOCK):
        p = p + inner[j] * u
        up_out[j] = p
        u = u + shift * p
        k = BLOCK - 1 - j
        down_out[k] = q
        w = w + shift * q
        q = q + inner[k] * w


def forward_y(received, table, ups, downs, weight, local, sums):
    value = received[...].reshape(BX, 2, 2, 16, 128)
    low, high = value[:, 0], value[:, 1]

    def lines(part):
        part = swap_blocks(part.reshape(BX * 2, 16, 128)).reshape(BX, 2, 16, 128)
        return jnp.concatenate([part[:, 0].reshape(64, 128), part[:, 1].reshape(64, 128)], 1)

    even = product(lines(low + high), table[0], table[1]).reshape(8, 8, M)
    odd = product(lines(low - high), table[2], table[3]).reshape(8, 8, M)
    mask = lower_half((8, 8, M))
    lower = jnp.where(mask, even, pltpu.roll(odd, 4, 1)).reshape(BX, 16, M)
    upper = jnp.where(mask, pltpu.roll(even, 4, 1), odd).reshape(BX, 16, M)
    scale = weight[...]
    rows = [(lower if j % 2 == 0 else upper)[j // 2] * scale for j in range(BLOCK)]
    above = [None] * BLOCK
    total_q = jnp.zeros((16, M), F32)
    for j in reversed(range(BLOCK)):
        above[j] = total_q
        total_q = total_q + downs[j] * rows[j]
    total_p = jnp.zeros((16, M), F32)
    for j in range(BLOCK):
        total_p = total_p + ups[j] * rows[j]
        local[j] = downs[j] * total_p + ups[j] * above[j]
    me = own_block()
    for n in range(BLOCKS):
        sums[n] = jnp.where(block_at(n) > me, total_p, total_q)


def inverse_y(local, ups, downs, sums, table, out):
    me = own_block()
    below = jnp.zeros((16, M), F32)
    above = jnp.zeros((16, M), F32)
    for n in range(BLOCKS):
        below = below + jnp.where(block_at(n) < me, sums[n], 0.0)
        above = above + jnp.where(block_at(n) > me, sums[n], 0.0)
    value = local[...] + downs[...] * below + ups[...] * above
    value = value.reshape(BX, 2, 16, M)
    lower, upper = value[:, 0].reshape(8, 8, M), value[:, 1].reshape(8, 8, M)
    mask = lower_half((8, 8, M))
    even = jnp.where(mask, lower, pltpu.roll(upper, 4, 1)).reshape(64, M)
    odd = jnp.where(mask, pltpu.roll(lower, 4, 1), upper).reshape(64, M)
    even = product(even, table[0], table[1])
    odd = product(odd, table[2], table[3])
    for half, part in enumerate((even + odd, even - odd)):
        for side in range(2):
            piece = part[:, side * 128 : (side + 1) * 128].reshape(BX, 16, 128)
            out[:, half, side] = swap_blocks(piece)


def shape(*dims):
    return jax.ShapeDtypeStruct(dims, F32)


VMEM = pl.BlockSpec(memory_space=pltpu.VMEM)
SMALL = pltpu.CompilerParams(vmem_limit_bytes=12 * 1024 * 1024)
HBM = pl.BlockSpec(memory_space=pltpu.HBM)


def on_device(source, faces):
    forward, inverse, eigen, eigen_y = (jnp.asarray(t) for t in tables())
    with jax.named_scope("forward_x"):
        operands = (source.reshape(64, N), forward, faces, eigen, eigen_y)
        half, ups, downs, weight, table = pl.pallas_call(
            forward_x,
            out_shape=(
                shape(M, 128),
                shape(BLOCK, 16, M),
                shape(BLOCK, 16, M),
                shape(16, M),
                jax.ShapeDtypeStruct((4, M, M), BF16),
            ),
            in_specs=[HBM] * 5,
            out_specs=(VMEM,) * 5,
            scratch_shapes=[
                pltpu.VMEM((64, N), F32),
                pltpu.SMEM((NZ + 1,), F32),
                pltpu.SMEM((N,), F32),
                pltpu.VMEM((16, M), F32),
                *[pltpu.VMEM((BLOCKS, 16, M), F32)] * 4,
                pltpu.SemaphoreType.DMA((5,)),
            ],
            compiler_params=SMALL,
        )(*[pltpu.with_memory_space_constraint(x, pltpu.HBM) for x in operands])
    with jax.named_scope("exchange_out"):
        pencils = lax.all_to_all(half.reshape(BX * HA, 4, 128), ("x2", "h"), 0, 0, tiled=True)
    with jax.named_scope("forward_y"):
        local, sums = pl.pallas_call(
            forward_y,
            out_shape=(shape(BLOCK, 16, M), shape(BLOCKS, 16, M)),
            in_specs=[VMEM] * 5,
            out_specs=(VMEM, VMEM),
            compiler_params=SMALL,
        )(pencils.reshape(M, 128), table, ups, downs, weight)
    with jax.named_scope("exchange_sums"):
        groups = [[y * NX + x for x in (k, NX - 1 - k) for y in range(NY)] for k in range(BX)]
        sums = lax.all_to_all(
            sums, ("y", "x1", "x2"), 0, 0, tiled=True, axis_index_groups=groups
        )
    with jax.named_scope("inverse_y"):
        back = pl.pallas_call(
            inverse_y,
            out_shape=shape(BX, 2, 2, 16, 128),
            in_specs=[VMEM] * 5,
            out_specs=VMEM,
            compiler_params=SMALL,
        )(local, ups, downs, sums, inverse)
    with jax.named_scope("exchange_back"):
        grid = lax.all_to_all(back.reshape(BX * HA, 4, 128), ("x2", "h"), 0, 0, tiled=True)
    with jax.named_scope("inverse_x"):
        out = pl.pallas_call(
            inverse_x,
            out_shape=shape(64, N),
            in_specs=[VMEM, VMEM],
            out_specs=VMEM,
            compiler_params=SMALL,
        )(grid.reshape(M, 128), inverse)
    return out.reshape(2, 32, N)


def solution(mesh):
    fine = Mesh(mesh.devices.reshape(NY, 2, BX, HA), ("y", "x1", "x2", "h"))
    spec = P(("y", "x1", "x2"), "h", None)
    return jax.shard_map(
        on_device, mesh=fine, in_specs=(spec, P()), out_specs=spec, check_vma=False
    )
```

```python
import math

import jax
import jax.numpy as jnp
import ml_dtypes
import numpy as np
from jax import lax
from jax.experimental import pallas as pl
from jax.experimental.pallas import tpu as pltpu
from jax.sharding import Mesh, PartitionSpec as P

N = 512
M = N // 2
NZ = 128
NY = 8
NX = 8
BX = 4
BLOCKS = NZ // (2 * BX)
BLOCK = NZ // BLOCKS
HA = 16
WAVES = N // (BX * HA)
F32 = jnp.float32
BF16 = jnp.bfloat16


def tables():
    j = np.arange(M)
    def cas(phase):
        t = 2.0 * np.pi * (phase % N) / N
        return (np.cos(t) + np.sin(t)) / math.sqrt(N)
    even = cas(2 * j[:, None] * j[None, :])
    odd = cas((2 * j[:, None] + 1) * j[None, :])
    def split(a):
        hi = a.astype(ml_dtypes.bfloat16)
        return [hi, (a - hi.astype(np.float64)).astype(ml_dtypes.bfloat16)]
    forward = np.stack(split(even) + split(odd.T))
    inverse = np.stack(split(even) + split(odd))
    eigen = 2.0 - 2.0 * np.cos(2.0 * np.pi * np.arange(N) / N)
    parity = (np.arange(16) // 4) % 2
    eigen_y = eigen[2 * j[None, :] + parity[:, None]]
    return forward, inverse, eigen.astype(np.float32), eigen_y.astype(np.float32)


def product(value, high, low):
    top = value.astype(BF16)
    rest = (value - top.astype(F32)).astype(BF16)
    rows = value.shape[0]
    both = jnp.dot(jnp.concatenate([top, rest], 0), high, preferred_element_type=F32)
    return both[:rows] + both[rows:] + jnp.dot(top, low, preferred_element_type=F32)


def swap_blocks(value):
    row = lax.broadcasted_iota(jnp.int32, value.shape, 1) // 4
    lane = lax.broadcasted_iota(jnp.int32, value.shape, 2) // 32
    far = pltpu.roll(pltpu.roll(value, 8, 1), 64, 2)
    value = jnp.where(((row ^ lane) & 2) == 0, value, far)
    near = pltpu.roll(value.reshape(-1, 8, 128), 4, 1).reshape(value.shape)
    near = jnp.where((lane & 1) == 0, pltpu.roll(near, 96, 2), pltpu.roll(near, 32, 2))
    return jnp.where(((row ^ lane) & 1) == 0, value, near)


def lower_half(shape):
    return lax.broadcasted_iota(jnp.int32, shape, 1) < 4


def place(index):
    return index + lax.axis_index("x1") * (BX - 1 - 2 * index)


def own_block():
    return 2 * lax.axis_index("y") + lax.axis_index("x1")


def block_at(position):
    return 2 * (position % NY) + position // NY


def forward_x(
    source, matrices, faces, eigen, eigen_y, out, up_out, down_out, weight_out, table,
    value, face, wave_x, wave_y, ps, us, qs, ws, sems,
):
    copies = [
        pltpu.make_async_copy(src, dst, sems.at[n])
        for n, (src, dst) in enumerate(
            ((faces, face), (eigen, wave_x), (eigen_y, wave_y), (source, value), (matrices, table))
        )
    ]
    for copy in copies:
        copy.start()
    for copy in copies[:3]:
        copy.wait()
    shift, blocks, inv = block_matrices(face, wave_x, wave_y)
    for copy in copies[3:]:
        copy.wait()
    left, right = value[:, :M], value[:, M:]
    even = product(left + right, table[0], table[1])
    odd = product(left - right, table[2], table[3])
    half = jnp.concatenate([even, odd], 0).T
    for share in range(BX):
        out[pl.ds(place(share) * 64, 64)] = half[share * 64 : (share + 1) * 64]
    coefficients(shift, blocks, inv, up_out, down_out, weight_out, ps, us, qs, ws)


def inverse_x(spectral, table, out):
    shares = [spectral[pl.ds(place(share) * 64, 64)] for share in range(BX)]
    value = jnp.concatenate(shares, 0).T
    even = product(value[:64], table[0], table[1])
    odd = product(value[64:], table[2], table[3])
    out[:, :M] = even + odd
    out[:, M:] = even - odd


def block_matrices(faces, eigen, eigen_y):
    first = WAVES * (place(lax.axis_index("x2")) * HA + lax.axis_index("h"))
    row = lax.broadcasted_iota(jnp.int32, (16, M), 0)
    wave = 2 * (row & 3) + (row >> 3)
    shift = eigen_y[...]
    for e in range(WAVES):
        shift = shift + jnp.where(wave == e, eigen[first + e], 0.0)

    def inv(index):
        part = 1.0 / jnp.full((8, 128), faces[index], F32)
        part = jnp.concatenate([part, part], 1)
        return jnp.concatenate([part, part], 0)

    blocks = [None] * BLOCKS
    for b in range(0, BLOCKS, 2):
        for c in (b, b + 1):
            g = inv(c * BLOCK)
            blocks[c] = (jnp.ones((16, M), F32), g, shift, 1.0 + shift * g)
        for j in range(1, BLOCK):
            for c in (b, b + 1):
                pa, pb, ua, ub = blocks[c]
                g = inv(c * BLOCK + j)
                pa, pb = pa + g * ua, pb + g * ub
                blocks[c] = (pa, pb, ua + shift * pa, ub + shift * pb)
    return shift, blocks, inv


def coefficients(shift, blocks, inv, up_out, down_out, weight_out, ps, us, qs, ws):
    last = inv(NZ)
    p, u = jnp.zeros((16, M), F32), jnp.ones((16, M), F32)
    q, w = last, jnp.ones((16, M), F32)
    for b in range(BLOCKS):
        ps[b], us[b] = p, u
        pa, pb, ua, ub = blocks[b]
        p, u = pa * p + pb * u, ua * p + ub * u
        c = BLOCKS - 1 - b
        qs[c], ws[c] = q, w
        pa, pb, ua, ub = blocks[c]
        q, w = ub * q + pb * w, ua * q + pa * w
    weight_out[...] = 1.0 / (p + last * u)

    me = own_block()
    inner = [inv(me * BLOCK + j) for j in range(BLOCK)]
    p, u, q, w = ps[me], us[me], qs[me], ws[me]
    for j in range(BLOCK):
        p = p + inner[j] * u
        up_out[j] = p
        u = u + shift * p
        k = BLOCK - 1 - j
        down_out[k] = q
        w = w + shift * q
        q = q + inner[k] * w


def forward_y(received, table, ups, downs, weight, local, sums):
    value = received[...].reshape(BX, 2, 2, 16, 128)
    low, high = value[:, 0], value[:, 1]

    def lines(part):
        part = swap_blocks(part.reshape(BX * 2, 16, 128)).reshape(BX, 2, 16, 128)
        return jnp.concatenate([part[:, 0].reshape(64, 128), part[:, 1].reshape(64, 128)], 1)

    even = product(lines(low + high), table[0], table[1]).reshape(8, 8, M)
    odd = product(lines(low - high), table[2], table[3]).reshape(8, 8, M)
    mask = lower_half((8, 8, M))
    lower = jnp.where(mask, even, pltpu.roll(odd, 4, 1)).reshape(BX, 16, M)
    upper = jnp.where(mask, pltpu.roll(even, 4, 1), odd).reshape(BX, 16, M)
    scale = weight[...]
    rows = [(lower if j % 2 == 0 else upper)[j // 2] * scale for j in range(BLOCK)]
    above = [None] * BLOCK
    total_q = jnp.zeros((16, M), F32)
    for j in reversed(range(BLOCK)):
        above[j] = total_q
        total_q = total_q + downs[j] * rows[j]
    total_p = jnp.zeros((16, M), F32)
    for j in range(BLOCK):
        total_p = total_p + ups[j] * rows[j]
        local[j] = downs[j] * total_p + ups[j] * above[j]
    me = own_block()
    for n in range(BLOCKS):
        sums[n] = jnp.where(block_at(n) > me, total_p, total_q)


def inverse_y(local, ups, downs, sums, table, out):
    me = own_block()
    below = jnp.zeros((16, M), F32)
    above = jnp.zeros((16, M), F32)
    for n in range(BLOCKS):
        below = below + jnp.where(block_at(n) < me, sums[n], 0.0)
        above = above + jnp.where(block_at(n) > me, sums[n], 0.0)
    value = local[...] + downs[...] * below + ups[...] * above
    value = value.reshape(BX, 2, 16, M)
    lower, upper = value[:, 0].reshape(8, 8, M), value[:, 1].reshape(8, 8, M)
    mask = lower_half((8, 8, M))
    even = jnp.where(mask, lower, pltpu.roll(upper, 4, 1)).reshape(64, M)
    odd = jnp.where(mask, pltpu.roll(lower, 4, 1), upper).reshape(64, M)
    even = product(even, table[0], table[1])
    odd = product(odd, table[2], table[3])
    for half, part in enumerate((even + odd, even - odd)):
        for side in range(2):
            piece = part[:, side * 128 : (side + 1) * 128].reshape(BX, 16, 128)
            out[:, half, side] = swap_blocks(piece)


def shape(*dims):
    return jax.ShapeDtypeStruct(dims, F32)


VMEM = pl.BlockSpec(memory_space=pltpu.VMEM)
SMALL = pltpu.CompilerParams(vmem_limit_bytes=12 * 1024 * 1024)
HBM = pl.BlockSpec(memory_space=pltpu.HBM)


def on_device(source, faces):
    forward, inverse, eigen, eigen_y = (jnp.asarray(t) for t in tables())
    with jax.named_scope("forward_x"):
        operands = (source.reshape(64, N), forward, faces, eigen, eigen_y)
        half, ups, downs, weight, table = pl.pallas_call(
            forward_x,
            out_shape=(
                shape(M, 128),
                shape(BLOCK, 16, M),
                shape(BLOCK, 16, M),
                shape(16, M),
                jax.ShapeDtypeStruct((4, M, M), BF16),
            ),
            in_specs=[HBM] * 5,
            out_specs=(VMEM,) * 5,
            scratch_shapes=[
                pltpu.VMEM((64, N), F32),
                pltpu.SMEM((NZ + 1,), F32),
                pltpu.SMEM((N,), F32),
                pltpu.VMEM((16, M), F32),
                *[pltpu.VMEM((BLOCKS, 16, M), F32)] * 4,
                pltpu.SemaphoreType.DMA((5,)),
            ],
            compiler_params=SMALL,
        )(*[pltpu.with_memory_space_constraint(x, pltpu.HBM) for x in operands])
    with jax.named_scope("exchange_out"):
        pencils = lax.all_to_all(half.reshape(BX * HA, 4, 128), ("x2", "h"), 0, 0, tiled=True)
    with jax.named_scope("forward_y"):
        local, sums = pl.pallas_call(
            forward_y,
            out_shape=(shape(BLOCK, 16, M), shape(BLOCKS, 16, M)),
            in_specs=[VMEM] * 5,
            out_specs=(VMEM, VMEM),
            compiler_params=SMALL,
        )(pencils.reshape(M, 128), table, ups, downs, weight)
    with jax.named_scope("exchange_sums"):
        groups = [[y * NX + x for x in (k, NX - 1 - k) for y in range(NY)] for k in range(BX)]
        sums = lax.all_to_all(
            sums, ("y", "x1", "x2"), 0, 0, tiled=True, axis_index_groups=groups
        )
    with jax.named_scope("inverse_y"):
        back = pl.pallas_call(
            inverse_y,
            out_shape=shape(BX, 2, 2, 16, 128),
            in_specs=[VMEM] * 5,
            out_specs=VMEM,
            compiler_params=SMALL,
        )(local, ups, downs, sums, inverse)
    with jax.named_scope("exchange_back"):
        grid = lax.all_to_all(back.reshape(BX * HA, 4, 128), ("x2", "h"), 0, 0, tiled=True)
    with jax.named_scope("inverse_x"):
        out = pl.pallas_call(
            inverse_x,
            out_shape=shape(64, N),
            in_specs=[VMEM, VMEM],
            out_specs=VMEM,
            compiler_params=SMALL,
        )(grid.reshape(M, 128), inverse)
    return out.reshape(2, 32, N)


def solution(mesh):
    fine = Mesh(mesh.devices.reshape(NY, 2, BX, HA), ("y", "x1", "x2", "h"))
    spec = P(("y", "x1", "x2"), "h", None)
    return jax.shard_map(
        on_device, mesh=fine, in_specs=(spec, P()), out_specs=spec, check_vma=False
    )
```

```python
import math

import jax
import jax.numpy as jnp
import ml_dtypes
import numpy as np
from jax import lax
from jax.experimental import pallas as pl
from jax.experimental.pallas import tpu as pltpu
from jax.sharding import Mesh, PartitionSpec as P

N = 512
M = N // 2
NZ = 128
NY = 8
NX = 8
BX = 4
BLOCKS = NZ // (2 * BX)
BLOCK = NZ // BLOCKS
HA = 16
WAVES = N // (BX * HA)
F32 = jnp.float32
BF16 = jnp.bfloat16


def tables():
    j = np.arange(M)
    def cas(phase):
        t = 2.0 * np.pi * (phase % N) / N
        return (np.cos(t) + np.sin(t)) / math.sqrt(N)
    even = cas(2 * j[:, None] * j[None, :])
    odd = cas((2 * j[:, None] + 1) * j[None, :])
    def split(a):
        hi = a.astype(ml_dtypes.bfloat16)
        return [hi, (a - hi.astype(np.float64)).astype(ml_dtypes.bfloat16)]
    forward = np.stack(split(even) + split(odd.T))
    inverse = np.stack(split(even) + split(odd))
    eigen = 2.0 - 2.0 * np.cos(2.0 * np.pi * np.arange(N) / N)
    parity = (np.arange(16) // 4) % 2
    eigen_y = eigen[2 * j[None, :] + parity[:, None]]
    return forward, inverse, eigen.astype(np.float32), eigen_y.astype(np.float32)


def product(value, high, low):
    top = value.astype(BF16)
    rest = (value - top.astype(F32)).astype(BF16)
    rows = value.shape[0]
    both = jnp.dot(jnp.concatenate([top, rest], 0), high, preferred_element_type=F32)
    return both[:rows] + both[rows:] + jnp.dot(top, low, preferred_element_type=F32)


def swap_blocks(value):
    row = lax.broadcasted_iota(jnp.int32, value.shape, 1) // 4
    lane = lax.broadcasted_iota(jnp.int32, value.shape, 2) // 32
    which = (row - lane) & 3
    out = value
    for s in range(1, 4):
        moved = pltpu.roll(pltpu.roll(value, 4 * s, 1), 128 - 32 * s, 2)
        out = jnp.where(which == s, moved, out)
    return out


def lower_half(shape):
    return lax.broadcasted_iota(jnp.int32, shape, 1) < 4


def place(index):
    return index + lax.axis_index("x1") * (BX - 1 - 2 * index)


def own_block():
    return 2 * lax.axis_index("y") + lax.axis_index("x1")


def block_at(position):
    return 4 * (position // 4) + 2 * (position % 2) + position // 2 % 2


def forward_x(
    source, matrices, faces, eigen, eigen_y, out, up_out, down_out, weight_out, table,
    value, face, wave_x, wave_y, ps, us, qs, ws, sems,
):
    copies = [
        pltpu.make_async_copy(src, dst, sems.at[n])
        for n, (src, dst) in enumerate(
            ((faces, face), (eigen, wave_x), (eigen_y, wave_y), (source, value), (matrices, table))
        )
    ]
    for copy in copies:
        copy.start()
    for copy in copies[:3]:
        copy.wait()
    shift, blocks, inv = block_matrices(face, wave_x, wave_y)
    for copy in copies[3:]:
        copy.wait()
    left, right = value[:, :M], value[:, M:]
    even = product(left + right, table[0], table[1])
    odd = product(left - right, table[2], table[3])
    half = jnp.concatenate([even, odd], 0).T
    for share in range(BX):
        out[pl.ds(place(share) * 64, 64)] = half[share * 64 : (share + 1) * 64]
    coefficients(shift, blocks, inv, up_out, down_out, weight_out, ps, us, qs, ws)


def inverse_x(spectral, table, out):
    shares = [spectral[pl.ds(place(share) * 64, 64)] for share in range(BX)]
    value = jnp.concatenate(shares, 0).T
    even = product(value[:64], table[0], table[1])
    odd = product(value[64:], table[2], table[3])
    out[:, :M] = even + odd
    out[:, M:] = even - odd


def block_matrices(faces, eigen, eigen_y):
    first = WAVES * (place(lax.axis_index("x2")) * HA + lax.axis_index("h"))
    row = lax.broadcasted_iota(jnp.int32, (16, M), 0)
    wave = 2 * (row & 3) + (row >> 3)
    shift = eigen_y[...]
    for e in range(WAVES):
        shift = shift + jnp.where(wave == e, eigen[first + e], 0.0)

    def inv(index):
        part = 1.0 / jnp.full((8, 128), faces[index], F32)
        part = jnp.concatenate([part, part], 1)
        return jnp.concatenate([part, part], 0)

    blocks = [None] * BLOCKS
    for b in range(0, BLOCKS, 2):
        for c in (b, b + 1):
            g = inv(c * BLOCK)
            blocks[c] = (jnp.ones((16, M), F32), g, shift, 1.0 + shift * g)
        for j in range(1, BLOCK):
            for c in (b, b + 1):
                pa, pb, ua, ub = blocks[c]
                g = inv(c * BLOCK + j)
                pa, pb = pa + g * ua, pb + g * ub
                blocks[c] = (pa, pb, ua + shift * pa, ub + shift * pb)
    return shift, blocks, inv


def coefficients(shift, blocks, inv, up_out, down_out, weight_out, ps, us, qs, ws):
    last = inv(NZ)
    p, u = jnp.zeros((16, M), F32), jnp.ones((16, M), F32)
    q, w = last, jnp.ones((16, M), F32)
    for b in range(BLOCKS):
        ps[b], us[b] = p, u
        pa, pb, ua, ub = blocks[b]
        p, u = pa * p + pb * u, ua * p + ub * u
        c = BLOCKS - 1 - b
        qs[c], ws[c] = q, w
        pa, pb, ua, ub = blocks[c]
        q, w = ub * q + pb * w, ua * q + pa * w
    weight_out[...] = 1.0 / (p + last * u)

    me = own_block()
    inner = [inv(me * BLOCK + j) for j in range(BLOCK)]
    p, u, q, w = ps[me], us[me], qs[me], ws[me]
    for j in range(BLOCK):
        p = p + inner[j] * u
        up_out[j] = p
        u = u + shift * p
        k = BLOCK - 1 - j
        down_out[k] = q
        w = w + shift * q
        q = q + inner[k] * w


def forward_y(received, table, ups, downs, weight, local, sums):
    value = received[...].reshape(BX, 2, 2, 16, 128)
    low, high = value[:, 0], value[:, 1]

    def lines(part):
        part = swap_blocks(part.reshape(BX * 2, 16, 128)).reshape(BX, 2, 16, 128)
        return jnp.concatenate([part[:, 0].reshape(64, 128), part[:, 1].reshape(64, 128)], 1)

    even = product(lines(low + high), table[0], table[1]).reshape(8, 8, M)
    odd = product(lines(low - high), table[2], table[3]).reshape(8, 8, M)
    mask = lower_half((8, 8, M))
    lower = jnp.where(mask, even, pltpu.roll(odd, 4, 1)).reshape(BX, 16, M)
    upper = jnp.where(mask, pltpu.roll(even, 4, 1), odd).reshape(BX, 16, M)
    scale = weight[...]
    rows = [(lower if j % 2 == 0 else upper)[j // 2] * scale for j in range(BLOCK)]
    above = [None] * BLOCK
    total_q = jnp.zeros((16, M), F32)
    for j in reversed(range(BLOCK)):
        above[j] = total_q
        total_q = total_q + downs[j] * rows[j]
    total_p = jnp.zeros((16, M), F32)
    for j in range(BLOCK):
        total_p = total_p + ups[j] * rows[j]
        local[j] = downs[j] * total_p + ups[j] * above[j]
    me = own_block()
    for n in range(BLOCKS):
        sums[n] = jnp.where(block_at(n) > me, total_p, total_q)


def inverse_y(local, ups, downs, sums, table, out):
    me = own_block()
    below = jnp.zeros((16, M), F32)
    above = jnp.zeros((16, M), F32)
    for n in range(BLOCKS):
        below = below + jnp.where(block_at(n) < me, sums[n], 0.0)
        above = above + jnp.where(block_at(n) > me, sums[n], 0.0)
    value = local[...] + downs[...] * below + ups[...] * above
    value = value.reshape(BX, 2, 16, M)
    lower, upper = value[:, 0].reshape(8, 8, M), value[:, 1].reshape(8, 8, M)
    mask = lower_half((8, 8, M))
    even = jnp.where(mask, lower, pltpu.roll(upper, 4, 1)).reshape(64, M)
    odd = jnp.where(mask, pltpu.roll(lower, 4, 1), upper).reshape(64, M)
    even = product(even, table[0], table[1])
    odd = product(odd, table[2], table[3])
    for half, part in enumerate((even + odd, even - odd)):
        for side in range(2):
            piece = part[:, side * 128 : (side + 1) * 128].reshape(BX, 16, 128)
            out[:, half, side] = swap_blocks(piece)


def shape(*dims):
    return jax.ShapeDtypeStruct(dims, F32)


VMEM = pl.BlockSpec(memory_space=pltpu.VMEM)
SMALL = pltpu.CompilerParams(vmem_limit_bytes=12 * 1024 * 1024)
HBM = pl.BlockSpec(memory_space=pltpu.HBM)


def on_device(source, faces):
    forward, inverse, eigen, eigen_y = (jnp.asarray(t) for t in tables())
    with jax.named_scope("forward_x"):
        operands = (source.reshape(64, N), forward, faces, eigen, eigen_y)
        half, ups, downs, weight, table = pl.pallas_call(
            forward_x,
            out_shape=(
                shape(M, 128),
                shape(BLOCK, 16, M),
                shape(BLOCK, 16, M),
                shape(16, M),
                jax.ShapeDtypeStruct((4, M, M), BF16),
            ),
            in_specs=[HBM] * 5,
            out_specs=(VMEM,) * 5,
            scratch_shapes=[
                pltpu.VMEM((64, N), F32),
                pltpu.SMEM((NZ + 1,), F32),
                pltpu.SMEM((N,), F32),
                pltpu.VMEM((16, M), F32),
                *[pltpu.VMEM((BLOCKS, 16, M), F32)] * 4,
                pltpu.SemaphoreType.DMA((5,)),
            ],
            compiler_params=SMALL,
        )(*[pltpu.with_memory_space_constraint(x, pltpu.HBM) for x in operands])
    with jax.named_scope("exchange_out"):
        pencils = lax.all_to_all(half.reshape(BX * HA, 4, 128), ("x2", "h"), 0, 0, tiled=True)
    with jax.named_scope("forward_y"):
        local, sums = pl.pallas_call(
            forward_y,
            out_shape=(shape(BLOCK, 16, M), shape(BLOCKS, 16, M)),
            in_specs=[VMEM] * 5,
            out_specs=(VMEM, VMEM),
            compiler_params=SMALL,
        )(pencils.reshape(M, 128), table, ups, downs, weight)
    with jax.named_scope("exchange_sums"):
        groups = [
            [(y + i) * NX + x for y in range(0, NY, 2) for x in (k, NX - 1 - k) for i in range(2)]
            for k in range(BX)
        ]
        sums = lax.all_to_all(
            sums, ("y", "x1", "x2"), 0, 0, tiled=True, axis_index_groups=groups
        )
    with jax.named_scope("inverse_y"):
        back = pl.pallas_call(
            inverse_y,
            out_shape=shape(BX, 2, 2, 16, 128),
            in_specs=[VMEM] * 5,
            out_specs=VMEM,
            compiler_params=SMALL,
        )(local, ups, downs, sums, inverse)
    with jax.named_scope("exchange_back"):
        grid = lax.all_to_all(back.reshape(BX * HA, 4, 128), ("x2", "h"), 0, 0, tiled=True)
    with jax.named_scope("inverse_x"):
        out = pl.pallas_call(
            inverse_x,
            out_shape=shape(64, N),
            in_specs=[VMEM, VMEM],
            out_specs=VMEM,
            compiler_params=SMALL,
        )(grid.reshape(M, 128), inverse)
    return out.reshape(2, 32, N)


def solution(mesh):
    fine = Mesh(mesh.devices.reshape(NY, 2, BX, HA), ("y", "x1", "x2", "h"))
    spec = P(("y", "x1", "x2"), "h", None)
    return jax.shard_map(
        on_device, mesh=fine, in_specs=(spec, P()), out_specs=spec, check_vma=False
    )
```

```python
import math

import jax
import jax.numpy as jnp
import ml_dtypes
import numpy as np
from jax import lax
from jax.experimental import pallas as pl
from jax.experimental.pallas import tpu as pltpu
from jax.sharding import Mesh, PartitionSpec as P

N = 512
M = N // 2
NZ = 128
NY = 8
NX = 8
BX = 4
BLOCKS = NZ // (2 * BX)
BLOCK = NZ // BLOCKS
HA = 16
WAVES = N // (BX * HA)
F32 = jnp.float32
BF16 = jnp.bfloat16


def tables():
    j = np.arange(M)
    def cas(phase):
        t = 2.0 * np.pi * (phase % N) / N
        return (np.cos(t) + np.sin(t)) / math.sqrt(N)
    even = cas(2 * j[:, None] * j[None, :])
    odd = cas((2 * j[:, None] + 1) * j[None, :])
    def split(a):
        hi = a.astype(ml_dtypes.bfloat16)
        return [hi, (a - hi.astype(np.float64)).astype(ml_dtypes.bfloat16)]
    forward = np.stack(split(even) + split(odd.T))
    inverse = np.stack(split(even) + split(odd))
    eigen = 2.0 - 2.0 * np.cos(2.0 * np.pi * np.arange(N) / N)
    parity = (np.arange(16) // 4) % 2
    eigen_y = eigen[2 * j[None, :] + parity[:, None]]
    return forward, inverse, eigen.astype(np.float32), eigen_y.astype(np.float32)


def product(value, high, low):
    top = value.astype(BF16)
    rest = (value - top.astype(F32)).astype(BF16)
    rows = value.shape[0]
    both = jnp.dot(jnp.concatenate([top, rest], 0), high, preferred_element_type=F32)
    return both[:rows] + both[rows:] + jnp.dot(top, low, preferred_element_type=F32)


def swap_blocks(value):
    row = lax.broadcasted_iota(jnp.int32, value.shape, 1) // 4
    lane = lax.broadcasted_iota(jnp.int32, value.shape, 2) // 32
    which = (row - lane) & 3
    out = value
    for s in range(1, 4):
        moved = pltpu.roll(pltpu.roll(value, 4 * s, 1), 128 - 32 * s, 2)
        out = jnp.where(which == s, moved, out)
    return out


def lower_half(shape):
    return lax.broadcasted_iota(jnp.int32, shape, 1) < 4


def place(index):
    return index + lax.axis_index("x1") * (BX - 1 - 2 * index)


def own_block():
    return 2 * lax.axis_index("y") + lax.axis_index("x1")


def block_at(position):
    return 2 * (position % NY) + position // NY


def forward_x(
    source, matrices, faces, eigen, eigen_y, out, up_out, down_out, weight_out, table,
    value, face, wave_x, wave_y, ps, us, qs, ws, sems,
):
    copies = [
        pltpu.make_async_copy(src, dst, sems.at[n])
        for n, (src, dst) in enumerate(
            ((faces, face), (eigen, wave_x), (eigen_y, wave_y), (source, value), (matrices, table))
        )
    ]
    for copy in copies:
        copy.start()
    for copy in copies[:3]:
        copy.wait()
    shift, blocks, inv = block_matrices(face, wave_x, wave_y)
    for copy in copies[3:]:
        copy.wait()
    left, right = value[:, :M], value[:, M:]
    even = product(left + right, table[0], table[1])
    odd = product(left - right, table[2], table[3])
    half = jnp.concatenate([even, odd], 0).T
    for share in range(BX):
        out[pl.ds(place(share) * 64, 64)] = half[share * 64 : (share + 1) * 64]
    coefficients(shift, blocks, inv, up_out, down_out, weight_out, ps, us, qs, ws)


def inverse_x(spectral, table, out):
    shares = [spectral[pl.ds(place(share) * 64, 64)] for share in range(BX)]
    value = jnp.concatenate(shares, 0).T
    even = product(value[:64], table[0], table[1])
    odd = product(value[64:], table[2], table[3])
    out[:, :M] = even + odd
    out[:, M:] = even - odd


def block_matrices(faces, eigen, eigen_y):
    first = WAVES * (place(lax.axis_index("x2")) * HA + lax.axis_index("h"))
    row = lax.broadcasted_iota(jnp.int32, (16, M), 0)
    wave = 2 * (row & 3) + (row >> 3)
    shift = eigen_y[...]
    for e in range(WAVES):
        shift = shift + jnp.where(wave == e, eigen[first + e], 0.0)

    def inv(index):
        part = pl.reciprocal(jnp.full((8, 128), faces[index], F32))
        part = jnp.concatenate([part, part], 1)
        return jnp.concatenate([part, part], 0)

    blocks = [None] * BLOCKS
    for b in range(0, BLOCKS, 2):
        for c in (b, b + 1):
            g = inv(c * BLOCK)
            blocks[c] = (jnp.ones((16, M), F32), g, shift, 1.0 + shift * g)
        for j in range(1, BLOCK):
            for c in (b, b + 1):
                pa, pb, ua, ub = blocks[c]
                g = inv(c * BLOCK + j)
                pa, pb = pa + g * ua, pb + g * ub
                blocks[c] = (pa, pb, ua + shift * pa, ub + shift * pb)
    return shift, blocks, inv


def coefficients(shift, blocks, inv, up_out, down_out, weight_out, ps, us, qs, ws):
    last = inv(NZ)
    p, u = jnp.zeros((16, M), F32), jnp.ones((16, M), F32)
    q, w = last, jnp.ones((16, M), F32)
    for b in range(BLOCKS):
        ps[b], us[b] = p, u
        pa, pb, ua, ub = blocks[b]
        p, u = pa * p + pb * u, ua * p + ub * u
        c = BLOCKS - 1 - b
        qs[c], ws[c] = q, w
        pa, pb, ua, ub = blocks[c]
        q, w = ub * q + pb * w, ua * q + pa * w
    weight_out[...] = pl.reciprocal(p + last * u)

    me = own_block()
    inner = [inv(me * BLOCK + j) for j in range(BLOCK)]
    p, u, q, w = ps[me], us[me], qs[me], ws[me]
    for j in range(BLOCK):
        p = p + inner[j] * u
        up_out[j] = p
        u = u + shift * p
        k = BLOCK - 1 - j
        down_out[k] = q
        w = w + shift * q
        q = q + inner[k] * w


def forward_y(received, table, ups, downs, weight, local, sums):
    value = received[...].reshape(BX, 2, 2, 16, 128)
    low, high = value[:, 0], value[:, 1]

    def lines(part):
        part = swap_blocks(part.reshape(BX * 2, 16, 128)).reshape(BX, 2, 16, 128)
        return jnp.concatenate([part[:, 0].reshape(64, 128), part[:, 1].reshape(64, 128)], 1)

    even = product(lines(low + high), table[0], table[1]).reshape(8, 8, M)
    odd = product(lines(low - high), table[2], table[3]).reshape(8, 8, M)
    mask = lower_half((8, 8, M))
    lower = jnp.where(mask, even, pltpu.roll(odd, 4, 1)).reshape(BX, 16, M)
    upper = jnp.where(mask, pltpu.roll(even, 4, 1), odd).reshape(BX, 16, M)
    scale = weight[...]
    rows = [(lower if j % 2 == 0 else upper)[j // 2] * scale for j in range(BLOCK)]
    above = [None] * BLOCK
    total_q = jnp.zeros((16, M), F32)
    for j in reversed(range(BLOCK)):
        above[j] = total_q
        total_q = total_q + downs[j] * rows[j]
    total_p = jnp.zeros((16, M), F32)
    for j in range(BLOCK):
        total_p = total_p + ups[j] * rows[j]
        local[j] = downs[j] * total_p + ups[j] * above[j]
    me = own_block()
    for n in range(BLOCKS):
        sums[n] = jnp.where(block_at(n) > me, total_p, total_q)


def inverse_y(local, ups, downs, sums, table, out):
    me = own_block()
    below = jnp.zeros((16, M), F32)
    above = jnp.zeros((16, M), F32)
    for n in range(BLOCKS):
        below = below + jnp.where(block_at(n) < me, sums[n], 0.0)
        above = above + jnp.where(block_at(n) > me, sums[n], 0.0)
    value = local[...] + downs[...] * below + ups[...] * above
    value = value.reshape(BX, 2, 16, M)
    lower, upper = value[:, 0].reshape(8, 8, M), value[:, 1].reshape(8, 8, M)
    mask = lower_half((8, 8, M))
    even = jnp.where(mask, lower, pltpu.roll(upper, 4, 1)).reshape(64, M)
    odd = jnp.where(mask, pltpu.roll(lower, 4, 1), upper).reshape(64, M)
    even = product(even, table[0], table[1])
    odd = product(odd, table[2], table[3])
    for half, part in enumerate((even + odd, even - odd)):
        for side in range(2):
            piece = part[:, side * 128 : (side + 1) * 128].reshape(BX, 16, 128)
            out[:, half, side] = swap_blocks(piece)


def shape(*dims):
    return jax.ShapeDtypeStruct(dims, F32)


VMEM = pl.BlockSpec(memory_space=pltpu.VMEM)
SMALL = pltpu.CompilerParams(vmem_limit_bytes=12 * 1024 * 1024)
HBM = pl.BlockSpec(memory_space=pltpu.HBM)


def on_device(source, faces):
    forward, inverse, eigen, eigen_y = (jnp.asarray(t) for t in tables())
    with jax.named_scope("forward_x"):
        operands = (source.reshape(64, N), forward, faces, eigen, eigen_y)
        half, ups, downs, weight, table = pl.pallas_call(
            forward_x,
            out_shape=(
                shape(M, 128),
                shape(BLOCK, 16, M),
                shape(BLOCK, 16, M),
                shape(16, M),
                jax.ShapeDtypeStruct((4, M, M), BF16),
            ),
            in_specs=[HBM] * 5,
            out_specs=(VMEM,) * 5,
            scratch_shapes=[
                pltpu.VMEM((64, N), F32),
                pltpu.SMEM((NZ + 1,), F32),
                pltpu.SMEM((N,), F32),
                pltpu.VMEM((16, M), F32),
                *[pltpu.VMEM((BLOCKS, 16, M), F32)] * 4,
                pltpu.SemaphoreType.DMA((5,)),
            ],
            compiler_params=SMALL,
        )(*[pltpu.with_memory_space_constraint(x, pltpu.HBM) for x in operands])
    with jax.named_scope("exchange_out"):
        pencils = lax.all_to_all(half.reshape(BX * HA, 4, 128), ("x2", "h"), 0, 0, tiled=True)
    with jax.named_scope("forward_y"):
        local, sums = pl.pallas_call(
            forward_y,
            out_shape=(shape(BLOCK, 16, M), shape(BLOCKS, 16, M)),
            in_specs=[VMEM] * 5,
            out_specs=(VMEM, VMEM),
            compiler_params=SMALL,
        )(pencils.reshape(M, 128), table, ups, downs, weight)
    with jax.named_scope("exchange_sums"):
        groups = [[y * NX + x for x in (k, NX - 1 - k) for y in range(NY)] for k in range(BX)]
        sums = lax.all_to_all(
            sums, ("y", "x1", "x2"), 0, 0, tiled=True, axis_index_groups=groups
        )
    with jax.named_scope("inverse_y"):
        back = pl.pallas_call(
            inverse_y,
            out_shape=shape(BX, 2, 2, 16, 128),
            in_specs=[VMEM] * 5,
            out_specs=VMEM,
            compiler_params=SMALL,
        )(local, ups, downs, sums, inverse)
    with jax.named_scope("exchange_back"):
        grid = lax.all_to_all(back.reshape(BX * HA, 4, 128), ("x2", "h"), 0, 0, tiled=True)
    with jax.named_scope("inverse_x"):
        out = pl.pallas_call(
            inverse_x,
            out_shape=shape(64, N),
            in_specs=[VMEM, VMEM],
            out_specs=VMEM,
            compiler_params=SMALL,
        )(grid.reshape(M, 128), inverse)
    return out.reshape(2, 32, N)


def solution(mesh):
    fine = Mesh(mesh.devices.reshape(NY, 2, BX, HA), ("y", "x1", "x2", "h"))
    spec = P(("y", "x1", "x2"), "h", None)
    return jax.shard_map(
        on_device, mesh=fine, in_specs=(spec, P()), out_specs=spec, check_vma=False
    )
```

```python
import math

import jax
import jax.numpy as jnp
import ml_dtypes
import numpy as np
from jax import lax
from jax.experimental import pallas as pl
from jax.experimental.pallas import tpu as pltpu
from jax.sharding import Mesh, PartitionSpec as P

N = 512
M = N // 2
NZ = 128
NY = 8
NX = 8
BX = 4
BLOCKS = NZ // (2 * BX)
BLOCK = NZ // BLOCKS
HA = 16
WAVES = N // (BX * HA)
F32 = jnp.float32
BF16 = jnp.bfloat16


def tables():
    j = np.arange(M)
    def cas(phase):
        t = 2.0 * np.pi * (phase % N) / N
        return (np.cos(t) + np.sin(t)) / math.sqrt(N)
    even = cas(2 * j[:, None] * j[None, :])
    odd = cas((2 * j[:, None] + 1) * j[None, :])
    def split(a):
        hi = a.astype(ml_dtypes.bfloat16)
        return [hi, (a - hi.astype(np.float64)).astype(ml_dtypes.bfloat16)]
    forward = np.stack(split(even) + split(odd.T))
    inverse = np.stack(split(even) + split(odd))
    eigen = 2.0 - 2.0 * np.cos(2.0 * np.pi * np.arange(N) / N)
    parity = (np.arange(16) // 4) % 2
    eigen_y = eigen[2 * j[None, :] + parity[:, None]]
    return forward, inverse, eigen.astype(np.float32), eigen_y.astype(np.float32)


def product(value, high, low):
    top = value.astype(BF16)
    rest = (value - top.astype(F32)).astype(BF16)
    rows = value.shape[0]
    both = jnp.dot(jnp.concatenate([top, rest], 0), high, preferred_element_type=F32)
    return both[:rows] + both[rows:] + jnp.dot(top, low, preferred_element_type=F32)


def swap_blocks(value):
    row = lax.broadcasted_iota(jnp.int32, value.shape, 1) // 4
    lane = lax.broadcasted_iota(jnp.int32, value.shape, 2) // 32
    which = (row - lane) & 3
    out = value
    for s in range(1, 4):
        moved = pltpu.roll(pltpu.roll(value, 4 * s, 1), 128 - 32 * s, 2)
        out = jnp.where(which == s, moved, out)
    return out


def lower_half(shape):
    return lax.broadcasted_iota(jnp.int32, shape, 1) < 4


def place(index):
    return index + lax.axis_index("x1") * (BX - 1 - 2 * index)


def own_block():
    return 2 * lax.axis_index("y") + lax.axis_index("x1")


def block_at(position):
    return 2 * (position % NY) + position // NY


def forward_x(
    source, matrices, faces, eigen, eigen_y, out, up_out, down_out, table,
    value, face, wave_x, wave_y, ps, us, qs, ws, sems,
):
    copies = [
        pltpu.make_async_copy(src, dst, sems.at[n])
        for n, (src, dst) in enumerate(
            ((faces, face), (eigen, wave_x), (eigen_y, wave_y), (source, value), (matrices, table))
        )
    ]
    for copy in copies:
        copy.start()
    for copy in copies[:3]:
        copy.wait()
    shift, blocks, inv = block_matrices(face, wave_x, wave_y)
    for copy in copies[3:]:
        copy.wait()
    left, right = value[:, :M], value[:, M:]
    even = product(left + right, table[0], table[1])
    odd = product(left - right, table[2], table[3])
    half = jnp.concatenate([even, odd], 0).T
    for share in range(BX):
        out[pl.ds(place(share) * 64, 64)] = half[share * 64 : (share + 1) * 64]
    coefficients(shift, blocks, inv, up_out, down_out, ps, us, qs, ws)


def inverse_x(spectral, table, out):
    shares = [spectral[pl.ds(place(share) * 64, 64)] for share in range(BX)]
    value = jnp.concatenate(shares, 0).T
    even = product(value[:64], table[0], table[1])
    odd = product(value[64:], table[2], table[3])
    out[:, :M] = even + odd
    out[:, M:] = even - odd


def block_matrices(faces, eigen, eigen_y):
    first = WAVES * (place(lax.axis_index("x2")) * HA + lax.axis_index("h"))
    row = lax.broadcasted_iota(jnp.int32, (16, M), 0)
    wave = 2 * (row & 3) + (row >> 3)
    shift = eigen_y[...]
    for e in range(WAVES):
        shift = shift + jnp.where(wave == e, eigen[first + e], 0.0)

    def inv(index):
        part = pl.reciprocal(jnp.full((8, 128), faces[index], F32))
        part = jnp.concatenate([part, part], 1)
        return jnp.concatenate([part, part], 0)

    blocks = [None] * BLOCKS
    for b in range(0, BLOCKS, 2):
        for c in (b, b + 1):
            g = inv(c * BLOCK)
            blocks[c] = (jnp.ones((16, M), F32), g, shift, 1.0 + shift * g)
        for j in range(1, BLOCK):
            for c in (b, b + 1):
                pa, pb, ua, ub = blocks[c]
                g = inv(c * BLOCK + j)
                pa, pb = pa + g * ua, pb + g * ub
                blocks[c] = (pa, pb, ua + shift * pa, ub + shift * pb)
    return shift, blocks, inv


def coefficients(shift, blocks, inv, up_out, down_out, ps, us, qs, ws):
    last = inv(NZ)
    p, u = jnp.zeros((16, M), F32), jnp.ones((16, M), F32)
    q, w = last, jnp.ones((16, M), F32)
    for b in range(BLOCKS):
        ps[b], us[b] = p, u
        pa, pb, ua, ub = blocks[b]
        p, u = pa * p + pb * u, ua * p + ub * u
        c = BLOCKS - 1 - b
        qs[c], ws[c] = q, w
        pa, pb, ua, ub = blocks[c]
        q, w = ub * q + pb * w, ua * q + pa * w
    weight = pl.reciprocal(p + last * u)

    me = own_block()
    inner = [inv(me * BLOCK + j) for j in range(BLOCK)]
    p, u, q, w = ps[me], us[me], qs[me] * weight, ws[me] * weight
    for j in range(BLOCK):
        p = p + inner[j] * u
        up_out[j] = p
        u = u + shift * p
        k = BLOCK - 1 - j
        down_out[k] = q
        w = w + shift * q
        q = q + inner[k] * w


def forward_y(received, table, ups, downs, local, sums):
    value = received[...].reshape(BX, 2, 2, 16, 128)
    low, high = value[:, 0], value[:, 1]

    def lines(part):
        part = swap_blocks(part.reshape(BX * 2, 16, 128)).reshape(BX, 2, 16, 128)
        return jnp.concatenate([part[:, 0].reshape(64, 128), part[:, 1].reshape(64, 128)], 1)

    even = product(lines(low + high), table[0], table[1]).reshape(8, 8, M)
    odd = product(lines(low - high), table[2], table[3]).reshape(8, 8, M)
    mask = lower_half((8, 8, M))
    lower = jnp.where(mask, even, pltpu.roll(odd, 4, 1)).reshape(BX, 16, M)
    upper = jnp.where(mask, pltpu.roll(even, 4, 1), odd).reshape(BX, 16, M)
    rows = [(lower if j % 2 == 0 else upper)[j // 2] for j in range(BLOCK)]
    above = [None] * BLOCK
    total_q = jnp.zeros((16, M), F32)
    for j in reversed(range(BLOCK)):
        above[j] = total_q
        total_q = total_q + downs[j] * rows[j]
    total_p = jnp.zeros((16, M), F32)
    for j in range(BLOCK):
        total_p = total_p + ups[j] * rows[j]
        local[j] = downs[j] * total_p + ups[j] * above[j]
    me = own_block()
    for n in range(BLOCKS):
        sums[n] = jnp.where(block_at(n) > me, total_p, total_q)


def inverse_y(local, ups, downs, sums, table, out):
    me = own_block()
    below = jnp.zeros((16, M), F32)
    above = jnp.zeros((16, M), F32)
    for n in range(BLOCKS):
        below = below + jnp.where(block_at(n) < me, sums[n], 0.0)
        above = above + jnp.where(block_at(n) > me, sums[n], 0.0)
    value = local[...] + downs[...] * below + ups[...] * above
    value = value.reshape(BX, 2, 16, M)
    lower, upper = value[:, 0].reshape(8, 8, M), value[:, 1].reshape(8, 8, M)
    mask = lower_half((8, 8, M))
    even = jnp.where(mask, lower, pltpu.roll(upper, 4, 1)).reshape(64, M)
    odd = jnp.where(mask, pltpu.roll(lower, 4, 1), upper).reshape(64, M)
    even = product(even, table[0], table[1])
    odd = product(odd, table[2], table[3])
    for half, part in enumerate((even + odd, even - odd)):
        for side in range(2):
            piece = part[:, side * 128 : (side + 1) * 128].reshape(BX, 16, 128)
            out[:, half, side] = swap_blocks(piece)


def shape(*dims):
    return jax.ShapeDtypeStruct(dims, F32)


VMEM = pl.BlockSpec(memory_space=pltpu.VMEM)
SMALL = pltpu.CompilerParams(vmem_limit_bytes=12 * 1024 * 1024)
HBM = pl.BlockSpec(memory_space=pltpu.HBM)


def on_device(source, faces):
    forward, inverse, eigen, eigen_y = (jnp.asarray(t) for t in tables())
    with jax.named_scope("forward_x"):
        operands = (source.reshape(64, N), forward, faces, eigen, eigen_y)
        half, ups, downs, table = pl.pallas_call(
            forward_x,
            out_shape=(
                shape(M, 128),
                shape(BLOCK, 16, M),
                shape(BLOCK, 16, M),
                jax.ShapeDtypeStruct((4, M, M), BF16),
            ),
            in_specs=[HBM] * 5,
            out_specs=(VMEM,) * 4,
            scratch_shapes=[
                pltpu.VMEM((64, N), F32),
                pltpu.SMEM((NZ + 1,), F32),
                pltpu.SMEM((N,), F32),
                pltpu.VMEM((16, M), F32),
                *[pltpu.VMEM((BLOCKS, 16, M), F32)] * 4,
                pltpu.SemaphoreType.DMA((5,)),
            ],
            compiler_params=SMALL,
        )(*[pltpu.with_memory_space_constraint(x, pltpu.HBM) for x in operands])
    with jax.named_scope("exchange_out"):
        pencils = lax.all_to_all(half.reshape(BX * HA, 4, 128), ("x2", "h"), 0, 0, tiled=True)
    with jax.named_scope("forward_y"):
        local, sums = pl.pallas_call(
            forward_y,
            out_shape=(shape(BLOCK, 16, M), shape(BLOCKS, 16, M)),
            in_specs=[VMEM] * 4,
            out_specs=(VMEM, VMEM),
            compiler_params=SMALL,
        )(pencils.reshape(M, 128), table, ups, downs)
    with jax.named_scope("exchange_sums"):
        groups = [[y * NX + x for x in (k, NX - 1 - k) for y in range(NY)] for k in range(BX)]
        sums = lax.all_to_all(
            sums, ("y", "x1", "x2"), 0, 0, tiled=True, axis_index_groups=groups
        )
    with jax.named_scope("inverse_y"):
        back = pl.pallas_call(
            inverse_y,
            out_shape=shape(BX, 2, 2, 16, 128),
            in_specs=[VMEM] * 5,
            out_specs=VMEM,
            compiler_params=SMALL,
        )(local, ups, downs, sums, inverse)
    with jax.named_scope("exchange_back"):
        grid = lax.all_to_all(back.reshape(BX * HA, 4, 128), ("x2", "h"), 0, 0, tiled=True)
    with jax.named_scope("inverse_x"):
        out = pl.pallas_call(
            inverse_x,
            out_shape=shape(64, N),
            in_specs=[VMEM, VMEM],
            out_specs=VMEM,
            compiler_params=SMALL,
        )(grid.reshape(M, 128), inverse)
    return out.reshape(2, 32, N)


def solution(mesh):
    fine = Mesh(mesh.devices.reshape(NY, 2, BX, HA), ("y", "x1", "x2", "h"))
    spec = P(("y", "x1", "x2"), "h", None)
    return jax.shard_map(
        on_device, mesh=fine, in_specs=(spec, P()), out_specs=spec, check_vma=False
    )
```

```python
import math

import jax
import jax.numpy as jnp
import ml_dtypes
import numpy as np
from jax import lax
from jax.experimental import pallas as pl
from jax.experimental.pallas import tpu as pltpu
from jax.sharding import Mesh, PartitionSpec as P

N = 512
M = N // 2
NZ = 128
NY = 8
NX = 8
BX = 4
BLOCKS = NZ // (2 * BX)
BLOCK = NZ // BLOCKS
HA = 16
WAVES = N // (BX * HA)
F32 = jnp.float32
BF16 = jnp.bfloat16


def tables():
    j = np.arange(M)
    def cas(phase):
        t = 2.0 * np.pi * (phase % N) / N
        return (np.cos(t) + np.sin(t)) / math.sqrt(N)
    even = cas(2 * j[:, None] * j[None, :])
    odd = cas((2 * j[:, None] + 1) * j[None, :])
    def split(a):
        hi = a.astype(ml_dtypes.bfloat16)
        return [hi, (a - hi.astype(np.float64)).astype(ml_dtypes.bfloat16)]
    forward = np.stack(split(even) + split(odd.T))
    inverse = np.stack(split(even) + split(odd))
    eigen = 2.0 - 2.0 * np.cos(2.0 * np.pi * np.arange(N) / N)
    parity = (np.arange(16) // 4) % 2
    eigen_y = eigen[2 * j[None, :] + parity[:, None]]
    return forward, inverse, eigen.astype(np.float32), eigen_y.astype(np.float32)


def product(value, high, low):
    top = value.astype(BF16)
    rest = (value - top.astype(F32)).astype(BF16)
    rows = value.shape[0]
    both = jnp.dot(jnp.concatenate([top, rest], 0), high, preferred_element_type=F32)
    return both[:rows] + both[rows:] + jnp.dot(top, low, preferred_element_type=F32)


def swap_blocks(value):
    row = lax.broadcasted_iota(jnp.int32, value.shape, 1) // 4
    lane = lax.broadcasted_iota(jnp.int32, value.shape, 2) // 32
    which = (row - lane) & 3
    out = value
    for s in range(1, 4):
        moved = pltpu.roll(pltpu.roll(value, 4 * s, 1), 128 - 32 * s, 2)
        out = jnp.where(which == s, moved, out)
    return out


def lower_half(shape):
    return lax.broadcasted_iota(jnp.int32, shape, 1) < 4


def place(index):
    return index + lax.axis_index("x1") * (BX - 1 - 2 * index)


def own_block():
    return 2 * lax.axis_index("y") + lax.axis_index("x1")


def block_at(position):
    return 2 * (position % NY) + position // NY


def forward_x(
    source, matrices, faces, eigen, eigen_y, out, up_out, down_out, table,
    value, face, wave_x, wave_y, ps, us, qs, ws, sems,
):
    copies = [
        pltpu.make_async_copy(src, dst, sems.at[n])
        for n, (src, dst) in enumerate(
            ((faces, face), (eigen, wave_x), (eigen_y, wave_y), (source, value), (matrices, table))
        )
    ]
    for copy in copies:
        copy.start()
    for copy in copies[:3]:
        copy.wait()
    shift, blocks, inv = block_matrices(face, wave_x, wave_y)
    for copy in copies[3:]:
        copy.wait()
    left, right = value[:, :M], value[:, M:]
    even = product(left + right, table[0], table[1])
    odd = product(left - right, table[2], table[3])
    half = jnp.concatenate([even, odd], 0).T
    for share in range(BX):
        out[pl.ds(place(share) * 64, 64)] = half[share * 64 : (share + 1) * 64]
    coefficients(shift, blocks, inv, up_out, down_out, ps, us, qs, ws)


def inverse_x(spectral, table, out):
    shares = [spectral[pl.ds(place(share) * 64, 64)] for share in range(BX)]
    value = jnp.concatenate(shares, 0).T
    even = product(value[:64], table[0], table[1])
    odd = product(value[64:], table[2], table[3])
    out[:, :M] = even + odd
    out[:, M:] = even - odd


def block_matrices(faces, eigen, eigen_y):
    first = WAVES * (place(lax.axis_index("x2")) * HA + lax.axis_index("h"))
    row = lax.broadcasted_iota(jnp.int32, (16, M), 0)
    wave = 2 * (row & 3) + (row >> 3)
    shift = eigen_y[...]
    for e in range(WAVES):
        shift = shift + jnp.where(wave == e, eigen[first + e], 0.0)

    def inv(index):
        part = pl.reciprocal(jnp.full((8, 128), faces[index], F32))
        part = jnp.concatenate([part, part], 1)
        return jnp.concatenate([part, part], 0)

    blocks = [None] * BLOCKS
    for b in range(0, BLOCKS, 4):
        for c in range(b, b + 4):
            g = inv(c * BLOCK)
            blocks[c] = (jnp.ones((16, M), F32), g, shift, 1.0 + shift * g)
        for j in range(1, BLOCK):
            for c in range(b, b + 4):
                pa, pb, ua, ub = blocks[c]
                g = inv(c * BLOCK + j)
                pa, pb = pa + g * ua, pb + g * ub
                blocks[c] = (pa, pb, ua + shift * pa, ub + shift * pb)
    return shift, blocks, inv


def coefficients(shift, blocks, inv, up_out, down_out, ps, us, qs, ws):
    last = inv(NZ)
    p, u = jnp.zeros((16, M), F32), jnp.ones((16, M), F32)
    q, w = last, jnp.ones((16, M), F32)
    for b in range(BLOCKS):
        ps[b], us[b] = p, u
        pa, pb, ua, ub = blocks[b]
        p, u = pa * p + pb * u, ua * p + ub * u
        c = BLOCKS - 1 - b
        qs[c], ws[c] = q, w
        pa, pb, ua, ub = blocks[c]
        q, w = ub * q + pb * w, ua * q + pa * w
    weight = pl.reciprocal(p + last * u)

    me = own_block()
    inner = [inv(me * BLOCK + j) for j in range(BLOCK)]
    p, u, q, w = ps[me], us[me], qs[me] * weight, ws[me] * weight
    for j in range(BLOCK):
        p = p + inner[j] * u
        up_out[j] = p
        u = u + shift * p
        k = BLOCK - 1 - j
        down_out[k] = q
        w = w + shift * q
        q = q + inner[k] * w


def forward_y(received, table, ups, downs, local, sums):
    value = received[...].reshape(BX, 2, 2, 16, 128)
    low, high = value[:, 0], value[:, 1]

    def lines(part):
        part = swap_blocks(part.reshape(BX * 2, 16, 128)).reshape(BX, 2, 16, 128)
        return jnp.concatenate([part[:, 0].reshape(64, 128), part[:, 1].reshape(64, 128)], 1)

    even = product(lines(low + high), table[0], table[1]).reshape(8, 8, M)
    odd = product(lines(low - high), table[2], table[3]).reshape(8, 8, M)
    mask = lower_half((8, 8, M))
    lower = jnp.where(mask, even, pltpu.roll(odd, 4, 1)).reshape(BX, 16, M)
    upper = jnp.where(mask, pltpu.roll(even, 4, 1), odd).reshape(BX, 16, M)
    rows = [(lower if j % 2 == 0 else upper)[j // 2] for j in range(BLOCK)]
    above = [None] * BLOCK
    total_q = jnp.zeros((16, M), F32)
    for j in reversed(range(BLOCK)):
        above[j] = total_q
        total_q = total_q + downs[j] * rows[j]
    total_p = jnp.zeros((16, M), F32)
    for j in range(BLOCK):
        total_p = total_p + ups[j] * rows[j]
        local[j] = downs[j] * total_p + ups[j] * above[j]
    me = own_block()
    for n in range(BLOCKS):
        sums[n] = jnp.where(block_at(n) > me, total_p, total_q)


def inverse_y(local, ups, downs, sums, table, out):
    me = own_block()
    below = jnp.zeros((16, M), F32)
    above = jnp.zeros((16, M), F32)
    for n in range(BLOCKS):
        below = below + jnp.where(block_at(n) < me, sums[n], 0.0)
        above = above + jnp.where(block_at(n) > me, sums[n], 0.0)
    value = local[...] + downs[...] * below + ups[...] * above
    value = value.reshape(BX, 2, 16, M)
    lower, upper = value[:, 0].reshape(8, 8, M), value[:, 1].reshape(8, 8, M)
    mask = lower_half((8, 8, M))
    even = jnp.where(mask, lower, pltpu.roll(upper, 4, 1)).reshape(64, M)
    odd = jnp.where(mask, pltpu.roll(lower, 4, 1), upper).reshape(64, M)
    even = product(even, table[0], table[1])
    odd = product(odd, table[2], table[3])
    for half, part in enumerate((even + odd, even - odd)):
        for side in range(2):
            piece = part[:, side * 128 : (side + 1) * 128].reshape(BX, 16, 128)
            out[:, half, side] = swap_blocks(piece)


def shape(*dims):
    return jax.ShapeDtypeStruct(dims, F32)


VMEM = pl.BlockSpec(memory_space=pltpu.VMEM)
SMALL = pltpu.CompilerParams(vmem_limit_bytes=12 * 1024 * 1024)
HBM = pl.BlockSpec(memory_space=pltpu.HBM)


def on_device(source, faces):
    forward, inverse, eigen, eigen_y = (jnp.asarray(t) for t in tables())
    with jax.named_scope("forward_x"):
        operands = (source.reshape(64, N), forward, faces, eigen, eigen_y)
        half, ups, downs, table = pl.pallas_call(
            forward_x,
            out_shape=(
                shape(M, 128),
                shape(BLOCK, 16, M),
                shape(BLOCK, 16, M),
                jax.ShapeDtypeStruct((4, M, M), BF16),
            ),
            in_specs=[HBM] * 5,
            out_specs=(VMEM,) * 4,
            scratch_shapes=[
                pltpu.VMEM((64, N), F32),
                pltpu.SMEM((NZ + 1,), F32),
                pltpu.SMEM((N,), F32),
                pltpu.VMEM((16, M), F32),
                *[pltpu.VMEM((BLOCKS, 16, M), F32)] * 4,
                pltpu.SemaphoreType.DMA((5,)),
            ],
            compiler_params=SMALL,
        )(*[pltpu.with_memory_space_constraint(x, pltpu.HBM) for x in operands])
    with jax.named_scope("exchange_out"):
        pencils = lax.all_to_all(half.reshape(BX * HA, 4, 128), ("x2", "h"), 0, 0, tiled=True)
    with jax.named_scope("forward_y"):
        local, sums = pl.pallas_call(
            forward_y,
            out_shape=(shape(BLOCK, 16, M), shape(BLOCKS, 16, M)),
            in_specs=[VMEM] * 4,
            out_specs=(VMEM, VMEM),
            compiler_params=SMALL,
        )(pencils.reshape(M, 128), table, ups, downs)
    with jax.named_scope("exchange_sums"):
        groups = [[y * NX + x for x in (k, NX - 1 - k) for y in range(NY)] for k in range(BX)]
        sums = lax.all_to_all(
            sums, ("y", "x1", "x2"), 0, 0, tiled=True, axis_index_groups=groups
        )
    with jax.named_scope("inverse_y"):
        back = pl.pallas_call(
            inverse_y,
            out_shape=shape(BX, 2, 2, 16, 128),
            in_specs=[VMEM] * 5,
            out_specs=VMEM,
            compiler_params=SMALL,
        )(local, ups, downs, sums, inverse)
    with jax.named_scope("exchange_back"):
        grid = lax.all_to_all(back.reshape(BX * HA, 4, 128), ("x2", "h"), 0, 0, tiled=True)
    with jax.named_scope("inverse_x"):
        out = pl.pallas_call(
            inverse_x,
            out_shape=shape(64, N),
            in_specs=[VMEM, VMEM],
            out_specs=VMEM,
            compiler_params=SMALL,
        )(grid.reshape(M, 128), inverse)
    return out.reshape(2, 32, N)


def solution(mesh):
    fine = Mesh(mesh.devices.reshape(NY, 2, BX, HA), ("y", "x1", "x2", "h"))
    spec = P(("y", "x1", "x2"), "h", None)
    return jax.shard_map(
        on_device, mesh=fine, in_specs=(spec, P()), out_specs=spec, check_vma=False
    )
```
